32 devices in a mesh: dp: 4 (over x, core), ctx: 8 (over z, y).
Axes of the slice: x: 2, y: 2, z: 4, core: 2. Of those that a mesh axis runs over, the one named last changes fastest.
Arguments:
- tokens: bfloat16 [4, 2048, 1024], P('dp', 'ctx'), may hold values from -6 to 6
- log_decay: float32 [4, 8, 2048], P('dp', None, 'ctx'), may hold values from -2.2 to 0
- lengths: int32 [4, 2], P('dp'), may hold values from 1 to 1280, 2048 in all within a row
- label_ids: int32 [4, 2048], P('dp', 'ctx'), may hold values from 0 to 511
- w_query: bfloat16 [1024, 1024], replicated, may hold values from -0.1875 to 0.1875
- w_key: bfloat16 [1024, 1024], replicated, may hold values from -0.1875 to 0.1875
- w_value: bfloat16 [1024, 1024], replicated, may hold values from -0.1875 to 0.1875
- norm_gain: float32 [1024], replicated, may hold values from 0.1 to 1.9
- label_query: bfloat16 [512, 1024], replicated, may hold values from -24 to 24
- label_weight: bfloat16 [512, 1024], replicated, may hold values from -0.75 to 0.75
Outputs:
- retention_out: bfloat16 [4, 2048, 1024], P('dp', 'ctx')
- logits: float32 [4, 2, 512], P('dp')
- recording_loss: float32 [4, 2], P('dp')
- mean_loss: float32 [], replicated
The draws below stay inside these ranges and needn't reach their ends.
Inputs may be any that keep to these rules, and one draw needn't show every extreme that they name: Row g lists the lengths of the 2 recordings packed in order into the 2048 tokens of group g; they sum to 2048.
All inputs are finite; a program needn't handle non-finite values.
Results may differ from the reference program's by a relative error of at most 0.0058.
The reference program's roundings to bfloat16 on the way count: a program that leaves them out, or rounds other values in their place, can miss the bound.
Values sent between devices are 32-bit elements; how exact they have to be, the bound alone decides.
A program may use at most 128 MiB of HBM per device.

```python
import math
import jax
import jax.numpy as jnp
import numpy as np
from jax import lax

D = 1024
H = 8
DH = 128
LABELS = 512
RECS = 2
TOK = 256
PACKED_GROUPS = 4
GROUP_TOKENS = 2048


def alignment_plan(key):
    pick_key = jax.random.fold_in(key, 701)
    sign_key = jax.random.fold_in(key, 702)
    label_key = jax.random.fold_in(key, 703)
    spot_rows = jax.random.randint(pick_key, (4,), 0, PACKED_GROUPS * GROUP_TOKENS - 1)
    sign_rows = (jax.random.randint(sign_key, (4, D), 0, 2) * 2 - 1).astype(jnp.float32)
    chosen = jax.random.permutation(label_key, LABELS)[:4]
    target_score = jnp.array([120.0, 160.0, 200.0, 250.0], jnp.float32)
    return (spot_rows, sign_rows, chosen, target_score)


def draw_tokens(key, part):
    base_key = jax.random.fold_in(key, 11)
    values = jnp.clip(jax.random.normal(base_key, (PACKED_GROUPS, GROUP_TOKENS, D), jnp.float32), -6.0, 6.0)
    spot_rows, sign_rows, chosen, target_score = alignment_plan(key)
    second_level = (4.0 - 8.0 / target_score)[:, None]
    flat_rows = values.reshape(PACKED_GROUPS * GROUP_TOKENS, D)
    flat_rows = flat_rows.at[spot_rows].set(4.0 * sign_rows)
    flat_rows = flat_rows.at[spot_rows + 1].set(second_level * sign_rows)
    values = flat_rows.reshape(PACKED_GROUPS, GROUP_TOKENS, D)
    return values.astype(jnp.bfloat16)


def draw_label_query(key, part):
    base_key = jax.random.fold_in(key, 21)
    values = jnp.clip(jax.random.normal(base_key, (LABELS, D), jnp.float32), -4.0, 4.0)
    spot_rows, sign_rows, chosen, target_score = alignment_plan(key)
    strength = target_score / (4.0 * jnp.sqrt(jnp.float32(DH)))
    values = values.at[chosen].set(strength[:, None] * sign_rows)
    return values.astype(jnp.bfloat16)


def draw_log_decay(key, part):
    power_key = jax.random.fold_in(key, 31)
    device_key = jax.random.fold_in(key, 32)
    token_key = jax.random.fold_in(key, 33)
    position_seed_key = jax.random.fold_in(key, 34)
    length_seed_key = jax.random.fold_in(key, 35)
    low_power = 5.3
    exponent = jax.random.uniform(power_key, (PACKED_GROUPS, H, 1, 1), jnp.float32, low_power, 13.0)
    rate_base = jnp.exp2(-exponent)
    device_factor = jnp.exp(jax.random.uniform(device_key, (PACKED_GROUPS, H, GROUP_TOKENS // TOK, 1), jnp.float32, jnp.log(0.6), jnp.log(1.5)))
    token_factor = jax.random.uniform(token_key, (PACKED_GROUPS, H, GROUP_TOKENS // TOK, TOK), jnp.float32, 0.5, 1.5)
    heart_rates = jnp.maximum(rate_base * device_factor * token_factor, 2.0 ** (-13))
    heart_rates = heart_rates.reshape(PACKED_GROUPS, H, GROUP_TOKENS)
    spike_position = jax.random.randint(position_seed_key, (PACKED_GROUPS, 3), 0, GROUP_TOKENS)
    spike_length = jax.random.uniform(length_seed_key, (PACKED_GROUPS, 3), jnp.float32, 0.2, 0.5)
    placed_value = jnp.arange(GROUP_TOKENS)[None, None, :] == spike_position[:, :, None]
    spike_addition = jnp.sum(jnp.where(placed_value, jnp.log1p(-spike_length)[:, :, None], 0.0), axis=1)
    return -heart_rates + spike_addition[:, None, :]


def set_ends(drawn, own_key, least, high):
    dims = drawn.shape
    spot = [jax.random.randint(jax.random.fold_in(own_key, axis), (), 0, dims[axis]) for axis in range(len(dims))]
    drawn = drawn.at[tuple(spot)].set(least)
    longest = dims.index(max(dims))
    spot[longest] = (spot[longest] + 1) % dims[longest]
    return drawn.at[tuple(spot)].set(high)


def rank_table(amount, skew):
    weights = [(1 << 20) // math.isqrt(grade ** skew) + 1 for grade in range(1, amount + 1)]
    spread = 1 + sum(weights) // (1 << 30)
    return np.cumsum(np.array([max(1, weight // spread) for weight in weights]))


def skewed_ids(stream_key, extent, number_of, slope):
    listing = rank_table(number_of, slope)
    pick = jax.random.randint(jax.random.fold_in(stream_key, 1), extent, 0, int(listing[number_of - 1]))
    standing = jnp.searchsorted(jnp.asarray(listing, jnp.int32), pick, side="right")
    return jax.random.permutation(jax.random.fold_in(stream_key, 2), number_of)[standing].astype(jnp.int32)


def length_profile(amount, total, most, lean):
    loads = [(1 << 20) // math.isqrt(rank ** lean) + 1 for rank in range(2, amount + 1)]
    spare, given = total - most - (amount - 1), [1] * (amount - 1)
    while spare > 0:
        movable = [i for i in range(amount - 1) if given[i] < most]
        pool, left = sum([loads[i] for i in movable]), spare
        for i in movable:
            addition = min(most - given[i], max(1, left * loads[i] // pool), spare)
            given[i] = given[i] + addition
            spare = spare - addition
    return np.array([most] + given)


def ragged(own_key, count, total, limit, slope):
    if count == 2:
        one = jax.random.randint(own_key, (), max(1, total - limit), min(limit, total - 1) + 1)
        return jnp.stack([one, total - one])
    sizes = jnp.asarray(length_profile(count, total, limit, slope), jnp.int32)
    twos = (count - 1) // 2
    source_of, taker = sizes[1:1 + 2 * twos:2], sizes[2:2 + 2 * twos:2]
    margin = jnp.minimum(source_of - 1, limit - taker)
    moved = jax.random.randint(jax.random.fold_in(own_key, 1), (twos,), 0, 1 << 20) % (margin + 1)
    sizes = sizes.at[1:1 + 2 * twos:2].set(source_of - moved).at[2:2 + 2 * twos:2].set(taker + moved)
    return sizes[jax.random.permutation(jax.random.fold_in(own_key, 2), count)]


def scatter_about(key, dims, spread, most, kind=jnp.bfloat16):
    return jnp.clip(spread * jax.random.normal(key, dims, jnp.float32), -most, most).astype(kind)


def setup_inputs(seed: int = 0) -> dict:
    seeds = jax.random.split(jax.random.key(seed), 11)
    tokens = draw_tokens(jax.random.fold_in(seeds[10], 71), 0)
    log_decay = draw_log_decay(jax.random.fold_in(seeds[10], 71), 0)
    lengths = jax.vmap(lambda own: ragged(own, RECS, GROUP_TOKENS, GROUP_TOKENS * 5 // 8, 2))(jax.random.split(seeds[2], PACKED_GROUPS)).reshape((PACKED_GROUPS, RECS)).astype(jnp.int32)
    label_ids = set_ends(skewed_ids(seeds[3], (PACKED_GROUPS, GROUP_TOKENS), LABELS, 2), jax.random.fold_in(seeds[3], 3), 0, LABELS - 1).astype(jnp.int32)
    w_query = scatter_about(seeds[4], (D, D), D ** -0.5, 0.1875)
    w_key = scatter_about(seeds[5], (D, D), D ** -0.5, 0.1875)
    w_value = scatter_about(seeds[6], (D, D), D ** -0.5, 0.1875)
    norm_gain = jnp.clip(1.0 + 0.18 * jax.random.normal(seeds[7], (D,), jnp.float32), 0.1, 1.9)
    label_query = draw_label_query(jax.random.fold_in(seeds[10], 71), 0)
    label_weight = scatter_about(seeds[9], (LABELS, D), (D // 16) ** -0.5, 0.75)
    return {"tokens": tokens, "log_decay": log_decay, "lengths": lengths, "label_ids": label_ids, "w_query": w_query, "w_key": w_key, "w_value": w_value, "norm_gain": norm_gain, "label_query": label_query, "label_weight": label_weight}


NEG_FILL = -1e+30

def record_ids(length_row, positions):
    starts = (jnp.cumsum(length_row) - length_row).astype(jnp.int32)
    return (lax.optimization_barrier(jnp.sum((starts[:, None] <= positions[None, :]).astype(jnp.int32), axis=0)) - 1).astype(jnp.int32)

def retention_block(state_all, block, w_query, w_key, w_value, norm_gain):
    features, decays, record, before_rec = block
    qk_scale = DH ** (-0.5)
    queries = jnp.dot(features, w_query, preferred_element_type=jnp.float32).astype(jnp.bfloat16)
    key_rows = jnp.dot(features, w_key, preferred_element_type=jnp.float32).astype(jnp.bfloat16)
    value_rows = jnp.dot(features, w_value, preferred_element_type=jnp.float32).astype(jnp.bfloat16)
    decay_cum = jnp.cumsum(decays, axis=1)
    local_pos = jnp.arange(TOK, dtype=jnp.int32)
    pair_mask = (local_pos[:, None] >= local_pos[None, :]) & (record[:, None] == record[None, :])
    linked = record == before_rec
    tail_rec = record == record[TOK - 1]

    def one_head(inputs):
        head_idx, state_head = inputs
        q_head = lax.dynamic_slice_in_dim(queries, head_idx * DH, DH, 1)
        k_head = lax.dynamic_slice_in_dim(key_rows, head_idx * DH, DH, 1)
        v_head = lax.dynamic_slice_in_dim(value_rows, head_idx * DH, DH, 1)
        cum_head = lax.dynamic_index_in_dim(decay_cum, head_idx, 0, keepdims=False)
        scores = jnp.dot(q_head, k_head.T, preferred_element_type=jnp.float32) * qk_scale
        decay_pair = jnp.exp(jnp.minimum(cum_head[:, None] - cum_head[None, :], 0.0))
        weights = jnp.where(pair_mask, scores * decay_pair, 0.0).astype(jnp.bfloat16)
        intra_sum = jnp.dot(weights, v_head, preferred_element_type=jnp.float32)
        k_decayed = (k_head.astype(jnp.float32) * jnp.where(tail_rec, jnp.exp(cum_head[TOK - 1] - cum_head), 0.0)[:, None]).astype(jnp.bfloat16)
        local_state = jnp.dot(k_decayed.T, v_head, preferred_element_type=jnp.float32)
        carry_factor = jnp.where(linked[TOK - 1], jnp.exp(cum_head[TOK - 1]), 0.0)
        q_decayed = q_head.astype(jnp.float32) * jnp.where(linked, jnp.exp(cum_head), 0.0)[:, None]
        total_out = intra_sum + jnp.dot(q_decayed, state_head, precision=lax.Precision.HIGH) * qk_scale
        centred = total_out - lax.optimization_barrier(jnp.mean(total_out, axis=1, keepdims=True))
        variance = lax.optimization_barrier(jnp.mean(centred * centred, axis=1, keepdims=True))
        gain_head = lax.dynamic_slice_in_dim(norm_gain, head_idx * DH, DH, 0)
        normed = centred * lax.rsqrt(variance + 1e-05) * gain_head[None, :]
        return (normed, carry_factor * state_head + local_state)
    normed, new_state = lax.map(one_head, (jnp.arange(H, dtype=jnp.int32), state_all))
    out_rows = jnp.transpose(normed, (1, 0, 2)).reshape(TOK, D).astype(jnp.bfloat16)
    return (new_state, out_rows)

def pool_group(features, out_rows, record, label_query, label_weight):
    qk_scale = DH ** (-0.5)

    def one_head(head_idx):
        k_head = lax.dynamic_slice_in_dim(features, head_idx * DH, DH, 1)
        q_label = lax.dynamic_slice_in_dim(label_query, head_idx * DH, DH, 1)
        y_head = lax.dynamic_slice_in_dim(out_rows, head_idx * DH, DH, 1)
        w_head = lax.dynamic_slice_in_dim(label_weight, head_idx * DH, DH, 1)
        scores = jnp.dot(q_label, k_head.T, preferred_element_type=jnp.float32) * qk_scale

        def record_max(rec_idx):
            return lax.optimization_barrier(jnp.max(jnp.where(record[None, :] == rec_idx, scores, NEG_FILL), axis=1))
        maxima = lax.map(record_max, jnp.arange(RECS, dtype=jnp.int32))
        pool_weight = jnp.exp(scores - maxima[record].T)
        label_value = jnp.dot(w_head, y_head.T, preferred_element_type=jnp.float32)
        mass_part = jax.ops.segment_sum(pool_weight.T, record, num_segments=RECS)
        weighted = jax.ops.segment_sum((pool_weight * label_value).T, record, num_segments=RECS)
        return weighted / mass_part
    return lax.optimization_barrier(jnp.sum(lax.map(one_head, jnp.arange(H, dtype=jnp.int32)), axis=0))

def reference(tokens, log_decay, lengths, label_ids, w_query, w_key, w_value, norm_gain, label_query, label_weight):
    blocks = GROUP_TOKENS // TOK
    positions = jnp.arange(GROUP_TOKENS, dtype=jnp.int32)
    out_list = []
    logit_list = []
    loss_list = []
    for group in range(PACKED_GROUPS):
        record = record_ids(lengths[group], positions)
        before_rec = jnp.concatenate([jnp.full((1,), -1, jnp.int32), record[TOK - 1::TOK][:blocks - 1].astype(jnp.int32)]).astype(jnp.int32)
        block_inputs = (tokens[group].reshape(blocks, TOK, D), jnp.transpose(log_decay[group].reshape(H, blocks, TOK), (1, 0, 2)), record.reshape(blocks, TOK), before_rec)

        def step_fn(state_all, block):
            return retention_block(state_all, block, w_query, w_key, w_value, norm_gain)
        final_state, out_blocks = lax.scan(step_fn, jnp.zeros((H, DH, DH), jnp.float32), block_inputs)
        out_rows = out_blocks.reshape(GROUP_TOKENS, D)
        logits = pool_group(tokens[group], out_rows, record, label_query, label_weight)
        counts = jnp.zeros((RECS, LABELS), jnp.float32).at[record, label_ids[group]].add(1.0)
        target = (counts + 0.5) / (lengths[group].astype(jnp.float32)[:, None] + 1.0)
        rec_loss = lax.optimization_barrier(jnp.mean(jax.nn.softplus(logits) - target * logits, axis=1))
        out_list.append(out_rows)
        logit_list.append(logits)
        loss_list.append(rec_loss)
    loss_all = jnp.stack(loss_list)
    mean_loss = jnp.sum(loss_all) / (PACKED_GROUPS * RECS)
    return (jnp.stack(out_list), jnp.stack(logit_list), loss_all, mean_loss)
```

```python
import functools
import math

import jax
import jax.numpy as jnp
from jax import lax
from jax.experimental import pallas as pl
from jax.experimental.pallas import tpu as pltpu
from jax.sharding import PartitionSpec as P

NEG_FILL = -1e30
LOG2E = math.log2(math.e)
F32 = jnp.float32
BF16 = jnp.bfloat16
NT = (((1,), (1,)), ((), ()))
TN = (((0,), (0,)), ((), ()))
PAD = 8


def fused(
    n,
    dp_n,
    lengths_ref,
    decay_ref,
    label_ref,
    gain_ref,
    tokens_hbm,
    wq_hbm,
    wk_hbm,
    wv_hbm,
    lq_hbm,
    lw_hbm,
    out_hbm,
    logits_ref,
    loss_ref,
    mean_ref,
    x_ref,
    wq_ref,
    wk_ref,
    wv_ref,
    lq_ref,
    lw_ref,
    q_ref,
    k_ref,
    v_ref,
    ccol,
    crow,
    pair_bias,
    intra,
    pool_w,
    weighted,
    out_buf,
    loc,
    peer_loc,
    chain_in,
    chain_out,
    hand,
    state,
    stats,
    stat_in,
    lse,
    contrib,
    contrib_in,
    loss_out,
    loss_in,
    in_sem,
    out_sem,
    loc_send,
    loc_recv,
    chain_send,
    chain_recv,
    hand_send,
    hand_recv,
    stat_send,
    stat_recv,
    lse_send,
    lse_recv,
    con_send,
    con_recv,
    dp_send,
    dp_recv,
):
    tok, width = x_ref.shape
    heads, _, hd = q_ref.shape
    labels = lq_ref.shape[0]
    recs = lengths_ref.shape[1]
    half_heads = heads // 2
    pairs = n // 2
    scale = hd ** (-0.5)
    soft = scale * LOG2E
    me = lax.axis_index("ctx")
    my_dp = lax.axis_index("dp")
    half = lax.rem(me, 2)
    pair = me // 2
    partner = me + 1 - 2 * half
    even = half == 0

    loads = [
        pltpu.make_async_copy(src, dst, in_sem.at[i])
        for i, (src, dst) in enumerate(
            (
                (tokens_hbm, x_ref),
                (wk_hbm, wk_ref),
                (wv_hbm, wv_ref),
                (wq_hbm, wq_ref),
                (lq_hbm, lq_ref),
                (lw_hbm, lw_ref),
            )
        )
    ]
    for load in loads:
        load.start()

    barrier = pltpu.get_barrier_semaphore()
    for d in range(1, n):
        pl.semaphore_signal(
            barrier,
            inc=1,
            device_id={"ctx": lax.rem(me + d, n)},
            device_id_type=pl.DeviceIdType.MESH,
        )
    for d in range(1, dp_n):
        pl.semaphore_signal(
            barrier,
            inc=1,
            device_id={"dp": lax.rem(my_dp + d, dp_n)},
            device_id_type=pl.DeviceIdType.MESH,
        )

    def send(src, dst, ssem, rsem, where):
        return pltpu.make_async_remote_copy(
            src_ref=src,
            dst_ref=dst,
            send_sem=ssem,
            recv_sem=rsem,
            device_id=where,
            device_id_type=pl.DeviceIdType.MESH,
        )

    shard_start = me * tok
    starts = []
    run = jnp.int32(0)
    for r in range(recs):
        starts.append(run)
        run = run + lengths_ref[0, r]

    def record_of(pos):
        rec = jnp.full_like(pos, -1)
        for r in range(recs):
            rec = rec + (starts[r] <= pos).astype(jnp.int32)
        return rec

    def record_scalar(pos):
        rec = jnp.int32(-1)
        for r in range(recs):
            rec = rec + (starts[r] <= pos).astype(jnp.int32)
        return rec

    before_rec = record_scalar(shard_start - 1)
    last_rec = record_scalar(shard_start + tok - 1)

    def col_record(lanes):
        return record_of(shard_start + lax.broadcasted_iota(jnp.int32, (tok, lanes), 0))

    def row_record(rows):
        return record_of(shard_start + lax.broadcasted_iota(jnp.int32, (rows, tok), 1))

    down = lax.broadcasted_iota(jnp.int32, (tok, tok), 0)
    across = lax.broadcasted_iota(jnp.int32, (tok, tok), 1)
    tri_low = (across <= down).astype(F32)
    decays = decay_ref[...]
    cum_rows = (
        lax.dot_general(
            decays, tri_low, NT, precision=lax.Precision.HIGHEST, preferred_element_type=F32
        )
        * LOG2E
    )
    cum_cols = (
        lax.dot_general(
            tri_low, decays, NT, precision=lax.Precision.HIGHEST, preferred_element_type=F32
        )
        * LOG2E
    )
    for h in range(heads):
        crow[h] = cum_rows[h : h + 1, :]
        ccol[h] = jnp.broadcast_to(cum_cols[:, h : h + 1], (tok, hd))
    pair_ok = (across <= down) & (col_record(tok) == row_record(tok))
    pair_bias[...] = jnp.where(pair_ok, math.log2(scale), NEG_FILL)

    def project(w_ref, dst):
        step = min(256, width)
        for c in range(width // step):
            res = jnp.dot(
                x_ref[...], w_ref[:, c * step : (c + 1) * step], preferred_element_type=F32
            ).astype(BF16)
            for s in range(step // hd):
                dst[c * (step // hd) + s] = res[:, s * hd : (s + 1) * hd]

    loads[0].wait()
    loads[1].wait()
    project(wk_ref, k_ref)
    loads[2].wait()
    project(wv_ref, v_ref)

    def local_state(h):
        cum = ccol[h]
        last = cum[tok - 1 : tok, :]
        fade = jnp.exp2(jnp.where(col_record(hd) == last_rec, last - cum, NEG_FILL))
        kdec = (k_ref[h].astype(F32) * fade).astype(BF16)
        loc[h, :hd, :] = lax.dot_general(kdec, v_ref[h], TN, preferred_element_type=F32)
        carry = jnp.where(last_rec == before_rec, jnp.exp2(last), 0.0)
        loc[h, hd:, :] = jnp.broadcast_to(carry, (PAD, hd))

    def loc_copy(i):
        h = (1 - half) * half_heads + i
        return send(
            loc.at[h], peer_loc.at[i], loc_send.at[i], loc_recv.at[i], {"ctx": partner}
        )

    pl.semaphore_wait(barrier, n - 1 + dp_n - 1)

    @pl.when(pair == 0)
    def _():
        chain_in[...] = jnp.zeros_like(chain_in)

    for i in range(half_heads):
        local_state((1 - half) * half_heads + i)
        loc_copy(i).start()
    for i in range(half_heads):
        local_state(half * half_heads + i)

    def chain_copy(i):
        return send(
            chain_out.at[i],
            chain_in.at[i],
            chain_send.at[i],
            chain_recv.at[i],
            {"ctx": lax.rem(me + 2, n)},
        )

    def hand_copy(i):
        return send(
            hand.at[i],
            state.at[half * half_heads + i],
            hand_send.at[i],
            hand_recv.at[i],
            {"ctx": partner},
        )

    def hand_arrival(i):
        return send(
            hand.at[i],
            state.at[(1 - half) * half_heads + i],
            hand_send.at[i],
            hand_recv.at[i],
            {"ctx": partner},
        )

    def chain_step(i):
        h = half * half_heads + i
        loc_copy(i).wait_recv()

        @pl.when(pair > 0)
        def _():
            chain_copy(i).wait_recv()

        came = chain_in[i]
        own = loc[h]
        other = peer_loc[i]
        first = jnp.where(even, own, other)
        second = jnp.where(even, other, own)
        middle = first[hd : hd + 1, :] * came + first[:hd, :]

        @pl.when(pair < pairs - 1)
        def _():
            chain_out[i] = second[hd : hd + 1, :] * middle + second[:hd, :]
            chain_copy(i).start()

        hand[i] = jnp.where(even, middle, came)
        hand_copy(i).start()
        state[h] = jnp.where(even, came, middle)

    units = 2 * heads
    first_unit = jnp.minimum(1 + 3 * pair, units - half_heads)

    def maybe_chain(unit):
        i = unit - first_unit

        @pl.when((i >= 0) & (i < half_heads))
        def _():
            chain_step(i)

    loads[3].wait()
    project(wq_ref, q_ref)
    loads[4].wait()

    chunk = min(256, labels)

    def pool_unit(h):
        lanes = pl.ds(pl.multiple_of(h * hd, hd), hd)
        rec = col_record(chunk)
        for c in range(labels // chunk):
            cols = slice(c * chunk, (c + 1) * chunk)
            scores = lax.dot_general(
                x_ref[:, lanes], lq_ref[cols, lanes], NT, preferred_element_type=F32
            )
            tops = [
                jnp.max(jnp.where(rec == r, scores, NEG_FILL), axis=0, keepdims=True)
                for r in range(recs)
            ]
            top = tops[0]
            for r in range(1, recs):
                top = jnp.where(rec == r, tops[r], top)
            weight = jnp.exp2((scores - top) * soft)
            pool_w[h, :, cols] = weight
            for r in range(recs):
                stats[h, r : r + 1, cols] = tops[r] * soft
                stats[h, recs + r : recs + r + 1, cols] = jnp.sum(
                    jnp.where(rec == r, weight, 0.0), axis=0, keepdims=True
                )

    def pool_body(h, _):
        pool_unit(h)
        maybe_chain(h)
        return 0

    lax.fori_loop(0, heads, pool_body, 0)

    def stat_copy(d):
        target = lax.rem(me + d, n)
        return target, send(
            stats.at[lax.rem(target, heads)],
            stat_in.at[me],
            stat_send.at[d],
            stat_recv.at[d],
            {"ctx": target},
        )

    def stat_arrival(d):
        return send(
            stats.at[0],
            stat_in.at[lax.rem(me - d + n, n)],
            stat_send.at[d],
            stat_recv.at[d],
            {"ctx": lax.rem(me + d, n)},
        )

    def each_peer(fn):
        for d in range(1, n):
            fn(d)

    def start_stat(d):
        target, copy = stat_copy(d)

        @pl.when(target < heads)
        def _():
            copy.start()

    each_peer(start_stat)

    def intra_unit(h):
        scores = lax.dot_general(q_ref[h], k_ref[h], NT, preferred_element_type=F32)
        cum = jnp.concatenate([ccol[h]] * (tok // hd), axis=1)
        fade = jnp.exp2(cum - crow[h] + pair_bias[...])
        weights = (scores * fade).astype(BF16)
        intra[h] = jnp.dot(weights, v_ref[h], preferred_element_type=F32)

    def intra_body(h, _):
        intra_unit(h)
        maybe_chain(heads + h)
        return 0

    lax.fori_loop(0, heads, intra_body, 0)

    def lse_copy(d):
        return send(
            lse.at[lax.rem(me, heads)],
            lse.at[lax.rem(me, heads)],
            lse_send.at[d],
            lse_recv.at[d],
            {"ctx": lax.rem(me + d, n)},
        )

    def lse_arrival(d):
        source = lax.rem(me - d + n, n)
        return source, send(
            lse.at[lax.rem(source, heads)],
            lse.at[lax.rem(source, heads)],
            lse_send.at[d],
            lse_recv.at[d],
            {"ctx": lax.rem(me + d, n)},
        )

    @pl.when(me < heads)
    def _():
        stat_in[me] = stats[lax.rem(me, heads)]
        each_peer(lambda d: stat_arrival(d).wait_recv())
        top = stat_in[0, :recs, :]
        for j in range(1, n):
            top = jnp.maximum(top, stat_in[j, :recs, :])
        mass = jnp.zeros_like(top)
        for j in range(n):
            mass = mass + stat_in[j, recs:, :] * jnp.exp2(stat_in[j, :recs, :] - top)
        lse[lax.rem(me, heads)] = top + jnp.log(mass) * LOG2E
        each_peer(lambda d: lse_copy(d).start())

    hot = (
        lax.broadcasted_iota(jnp.int32, (labels, tok), 0) == label_ref[...]
    ).astype(F32).astype(BF16)
    members = (
        row_record(16) == lax.broadcasted_iota(jnp.int32, (16, tok), 0)
    ).astype(F32).astype(BF16)
    counts = lax.dot_general(members, hot, NT, preferred_element_type=F32)
    contrib[recs:, :] = counts[:recs, :]

    loads[5].wait()

    def finish(h):
        lanes = pl.ds(pl.multiple_of(h * hd, hd), hd)
        st = state[h]
        high = st.astype(BF16)
        low = (st - high.astype(F32)).astype(BF16)
        q = q_ref[h]
        inter = jnp.dot(
            jnp.concatenate([q, q], axis=1),
            jnp.concatenate([high, low], axis=0),
            preferred_element_type=F32,
        )
        fade = jnp.exp2(
            jnp.where(col_record(hd) == before_rec, ccol[h] + math.log2(scale), NEG_FILL)
        )
        total = intra[h] + inter * fade
        centred = total - jnp.mean(total, axis=1, keepdims=True)
        variance = jnp.mean(centred * centred, axis=1, keepdims=True)
        rows = (centred * lax.rsqrt(variance + 1e-05) * gain_ref[pl.ds(h, 1), :]).astype(BF16)
        out_buf[:, lanes] = rows
        rec = col_record(chunk)
        for c in range(labels // chunk):
            cols = slice(c * chunk, (c + 1) * chunk)
            value = lax.dot_general(rows, lw_ref[cols, lanes], NT, preferred_element_type=F32)
            value = value * pool_w[h, :, cols]
            for r in range(recs):
                weighted[h, r : r + 1, cols] = jnp.sum(
                    jnp.where(rec == r, value, 0.0), axis=0, keepdims=True
                )

    def finish_own(i, _):
        finish(half * half_heads + i)
        return 0

    def finish_other(i, _):
        hand_arrival(i).wait_recv()
        finish((1 - half) * half_heads + i)
        return 0

    lax.fori_loop(0, half_heads, finish_own, 0)
    lax.fori_loop(0, half_heads, finish_other, 0)

    store = pltpu.make_async_copy(out_buf, out_hbm, out_sem)
    store.start()

    def wait_lse(d):
        source, copy = lse_arrival(d)

        @pl.when(source < heads)
        def _():
            copy.wait_recv()

    each_peer(wait_lse)
    part = jnp.zeros((recs, labels), F32)
    for h in range(heads):
        part = part + weighted[h] * jnp.exp2(stats[h, :recs, :] - lse[h])
    contrib[:recs, :] = part

    def con_copy(d):
        return send(
            contrib,
            contrib_in.at[d],
            con_send.at[d],
            con_recv.at[d],
            {"ctx": lax.rem(me + d, n)},
        )

    each_peer(lambda d: con_copy(d).start())
    contrib_in[0] = contrib[...]
    each_peer(lambda d: con_copy(d).wait_recv())
    both = contrib_in[lax.rem(me, n)]
    for j in range(1, n):
        both = both + contrib_in[lax.rem(me - j + n, n)]
    logits = both[:recs, :]
    logits_ref[...] = logits
    losses = []
    total_loss = jnp.zeros((1, 1), F32)
    for r in range(recs):
        z = logits[r : r + 1, :]
        target = (both[recs + r : recs + r + 1, :] + 0.5) / (
            lengths_ref[0, r].astype(F32) + 1.0
        )
        soft_plus = jnp.maximum(z, 0.0) + jnp.log1p(jnp.exp(-jnp.abs(z)))
        value = jnp.mean(soft_plus - target * z, axis=1, keepdims=True)
        losses.append(value)
        total_loss = total_loss + value
    spot = lax.broadcasted_iota(jnp.int32, (1, recs), 1)
    row = jnp.zeros((1, recs), F32)
    for r in range(recs):
        row = jnp.where(spot == r, losses[r], row)
    loss_ref[...] = row
    loss_out[...] = jnp.broadcast_to(total_loss, loss_out.shape)

    def dp_copy(d):
        return send(
            loss_out,
            loss_in.at[d],
            dp_send.at[d],
            dp_recv.at[d],
            {"dp": lax.rem(my_dp + d, dp_n)},
        )

    for d in range(1, dp_n):
        dp_copy(d).start()
    loss_in[0] = loss_out[...]
    for d in range(1, dp_n):
        dp_copy(d).wait_recv()
    total = loss_in[lax.rem(my_dp, dp_n)]
    for j in range(1, dp_n):
        total = total + loss_in[lax.rem(my_dp - j + dp_n, dp_n)]
    mean_ref[...] = total[:1, :1] / (dp_n * recs)

    for d in range(1, dp_n):
        dp_copy(d).wait_send()
    each_peer(lambda d: con_copy(d).wait_send())

    @pl.when(me < heads)
    def _():
        each_peer(lambda d: lse_copy(d).wait_send())

    def end_stat(d):
        target, copy = stat_copy(d)

        @pl.when(target < heads)
        def _():
            copy.wait_send()

    each_peer(end_stat)
    for i in range(half_heads):
        loc_copy(i).wait_send()
        hand_copy(i).wait_send()

    @pl.when(pair < pairs - 1)
    def _():
        for i in range(half_heads):
            chain_copy(i).wait_send()

    store.wait()


def local(
    tokens,
    log_decay,
    lengths,
    label_ids,
    w_query,
    w_key,
    w_value,
    norm_gain,
    label_query,
    label_weight,
):
    n = lax.axis_size("ctx")
    dp_n = lax.axis_size("dp")
    tok, width = tokens.shape[1:]
    heads = log_decay.shape[1]
    hd = width // heads
    recs = lengths.shape[1]
    labels = label_query.shape[0]
    half = heads // 2
    assert n >= heads and n % 2 == 0
    any_space = pl.BlockSpec(memory_space=pl.ANY)
    vmem = pl.BlockSpec(memory_space=pltpu.VMEM)
    smem = pl.BlockSpec(memory_space=pltpu.SMEM)
    dma = pltpu.SemaphoreType.DMA
    out, logits, loss, mean = pl.pallas_call(
        functools.partial(fused, n, dp_n),
        out_shape=(
            jax.ShapeDtypeStruct((tok, width), BF16),
            jax.ShapeDtypeStruct((recs, labels), F32),
            jax.ShapeDtypeStruct((1, recs), F32),
            jax.ShapeDtypeStruct((1, 1), F32),
        ),
        in_specs=[smem, vmem, vmem, vmem] + [any_space] * 6,
        out_specs=(any_space, vmem, vmem, vmem),
        scratch_shapes=[
            pltpu.VMEM((tok, width), BF16),
            pltpu.VMEM((width, width), BF16),
            pltpu.VMEM((width, width), BF16),
            pltpu.VMEM((width, width), BF16),
            pltpu.VMEM((labels, width), BF16),
            pltpu.VMEM((labels, width), BF16),
            pltpu.VMEM((heads, tok, hd), BF16),
            pltpu.VMEM((heads, tok, hd), BF16),
            pltpu.VMEM((heads, tok, hd), BF16),
            pltpu.VMEM((heads, tok, hd), F32),
            pltpu.VMEM((heads, 1, tok), F32),
            pltpu.VMEM((tok, tok), F32),
            pltpu.VMEM((heads, tok, hd), F32),
            pltpu.VMEM((heads, tok, labels), F32),
            pltpu.VMEM((heads, recs, labels), F32),
            pltpu.VMEM((tok, width), BF16),
            pltpu.VMEM((heads, hd + PAD, hd), F32),
            pltpu.VMEM((half, hd + PAD, hd), F32),
            pltpu.VMEM((half, hd, hd), F32),
            pltpu.VMEM((half, hd, hd), F32),
            pltpu.VMEM((half, hd, hd), F32),
            pltpu.VMEM((heads, hd, hd), F32),
            pltpu.VMEM((heads, 2 * recs, labels), F32),
            pltpu.VMEM((n, 2 * recs, labels), F32),
            pltpu.VMEM((heads, recs, labels), F32),
            pltpu.VMEM((2 * recs, labels), F32),
            pltpu.VMEM((n, 2 * recs, labels), F32),
            pltpu.VMEM((8, 128), F32),
            pltpu.VMEM((dp_n, 8, 128), F32),
            dma((6,)),
            dma,
            dma((half,)),
            dma((half,)),
            dma((half,)),
            dma((half,)),
            dma((half,)),
            dma((half,)),
            dma((n,)),
            dma((n,)),
            dma((n,)),
            dma((n,)),
            dma((n,)),
            dma((n,)),
            dma((dp_n,)),
            dma((dp_n,)),
        ],
        compiler_params=pltpu.CompilerParams(
            collective_id=0, has_side_effects=True, vmem_limit_bytes=48 * 1024 * 1024
        ),
    )(
        lengths,
        log_decay[0],
        label_ids,
        norm_gain.reshape(heads, hd),
        tokens[0],
        w_query,
        w_key,
        w_value,
        label_query,
        label_weight,
    )
    return (out[None], logits[None], loss, mean.reshape(()))


def solution(mesh):
    return jax.shard_map(
        local,
        mesh=mesh,
        in_specs=(
            P("dp", "ctx", None),
            P("dp", None, "ctx"),
            P("dp", None),
            P("dp", "ctx"),
            P(),
            P(),
            P(),
            P(),
            P(),
            P(),
        ),
        out_specs=(P("dp", "ctx", None), P("dp", None, None), P("dp", None), P()),
        check_vma=False,
    )
```

```python
import functools
import math

import jax
import jax.numpy as jnp
from jax import lax
from jax.experimental import pallas as pl
from jax.experimental.pallas import tpu as pltpu
from jax.sharding import PartitionSpec as P

NEG_FILL = -1e30
LOG2E = math.log2(math.e)
F32 = jnp.float32
BF16 = jnp.bfloat16
NT = (((1,), (1,)), ((), ()))
TN = (((0,), (0,)), ((), ()))
PAD = 8
VMEM_LIMIT = 63 * 1024 * 1024


def fused(
    n,
    dp_n,
    lengths_hbm,
    decay_hbm,
    label_hbm,
    gain_hbm,
    tokens_hbm,
    wq_hbm,
    wk_hbm,
    wv_hbm,
    lq_hbm,
    lw_hbm,
    out_hbm,
    logits_ref,
    loss_ref,
    mean_ref,
    lengths_ref,
    decay_ref,
    label_ref,
    gain_ref,
    x_ref,
    wq_ref,
    wk_ref,
    wv_ref,
    lq_ref,
    lw_ref,
    q_ref,
    k_ref,
    v_ref,
    ccol,
    crow,
    pair_bias,
    intra,
    pool_w,
    weighted,
    out_buf,
    loc,
    peer_loc,
    chain_in,
    chain_out,
    hand,
    state,
    stats,
    stat_in,
    lse,
    contrib,
    contrib_in,
    loss_out,
    loss_in,
    in_sem,
    out_sem,
    loc_send,
    loc_recv,
    chain_send,
    chain_recv,
    hand_send,
    hand_recv,
    stat_send,
    stat_recv,
    lse_send,
    lse_recv,
    con_send,
    con_recv,
    dp_send,
    dp_recv,
):
    tok, width = x_ref.shape
    heads, _, hd = q_ref.shape
    labels = lq_ref.shape[0]
    recs = lengths_ref.shape[1]
    half_heads = heads // 2
    pairs = n // 2
    scale = hd ** (-0.5)
    soft = scale * LOG2E
    me = lax.axis_index("ctx")
    my_dp = lax.axis_index("dp")
    half = lax.rem(me, 2)
    pair = me // 2
    partner = me + 1 - 2 * half
    even = half == 0

    part = half_heads * hd
    far_cols = pl.ds(pl.multiple_of((1 - half) * part, part), part)
    near_cols = pl.ds(pl.multiple_of(half * part, part), part)
    plan = (
        (lengths_hbm, lengths_ref),
        (decay_hbm, decay_ref),
        (tokens_hbm, x_ref),
        (wk_hbm.at[:, far_cols], wk_ref.at[0]),
        (wv_hbm.at[:, far_cols], wv_ref.at[0]),
        (wk_hbm.at[:, near_cols], wk_ref.at[1]),
        (wv_hbm.at[:, near_cols], wv_ref.at[1]),
        (wq_hbm, wq_ref),
        (lq_hbm, lq_ref),
        (lw_hbm, lw_ref),
        (label_hbm, label_ref),
        (gain_hbm, gain_ref),
    )
    loads = [pltpu.make_async_copy(src, dst, in_sem.at[i]) for i, (src, dst) in enumerate(plan)]
    for load in loads:
        load.start()

    barrier = pltpu.get_barrier_semaphore()
    for d in range(1, n):
        pl.semaphore_signal(
            barrier,
            inc=1,
            device_id={"ctx": lax.rem(me + d, n)},
            device_id_type=pl.DeviceIdType.MESH,
        )
    for d in range(1, dp_n):
        pl.semaphore_signal(
            barrier,
            inc=1,
            device_id={"dp": lax.rem(my_dp + d, dp_n)},
            device_id_type=pl.DeviceIdType.MESH,
        )

    def send(src, dst, ssem, rsem, where):
        return pltpu.make_async_remote_copy(
            src_ref=src,
            dst_ref=dst,
            send_sem=ssem,
            recv_sem=rsem,
            device_id=where,
            device_id_type=pl.DeviceIdType.MESH,
        )

    loads[0].wait()
    loads[1].wait()
    shard_start = me * tok
    starts = []
    run = jnp.int32(0)
    for r in range(recs):
        starts.append(run)
        run = run + lengths_ref[0, r]

    def record_of(pos):
        rec = jnp.full_like(pos, -1)
        for r in range(recs):
            rec = rec + (starts[r] <= pos).astype(jnp.int32)
        return rec

    def record_scalar(pos):
        rec = jnp.int32(-1)
        for r in range(recs):
            rec = rec + (starts[r] <= pos).astype(jnp.int32)
        return rec

    before_rec = record_scalar(shard_start - 1)
    last_rec = record_scalar(shard_start + tok - 1)

    def col_record(lanes):
        return record_of(shard_start + lax.broadcasted_iota(jnp.int32, (tok, lanes), 0))

    def row_record(rows):
        return record_of(shard_start + lax.broadcasted_iota(jnp.int32, (rows, tok), 1))

    down = lax.broadcasted_iota(jnp.int32, (tok, tok), 0)
    across = lax.broadcasted_iota(jnp.int32, (tok, tok), 1)
    tri_low = (across <= down).astype(F32)
    decays = decay_ref[...]
    cum_rows = (
        lax.dot_general(
            decays, tri_low, NT, precision=lax.Precision.HIGHEST, preferred_element_type=F32
        )
        * LOG2E
    )
    cum_cols = (
        lax.dot_general(
            tri_low, decays, NT, precision=lax.Precision.HIGHEST, preferred_element_type=F32
        )
        * LOG2E
    )
    for h in range(heads):
        crow[h] = cum_rows[h : h + 1, :]
        ccol[h] = jnp.broadcast_to(cum_cols[:, h : h + 1], (tok, hd))
    pair_ok = (across <= down) & (col_record(tok) == row_record(tok))
    pair_bias[...] = jnp.where(pair_ok, math.log2(scale), NEG_FILL)

    def project(w_ref, dst, first):
        columns = w_ref.shape[1]
        step = min(256, columns)
        for c in range(columns // step):
            res = jnp.dot(
                x_ref[...], w_ref[:, c * step : (c + 1) * step], preferred_element_type=F32
            ).astype(BF16)
            for s in range(step // hd):
                dst[first + c * (step // hd) + s] = res[:, s * hd : (s + 1) * hd]

    def local_state(h):
        cum = ccol[h]
        last = cum[tok - 1 : tok, :]
        fade = jnp.exp2(jnp.where(col_record(hd) == last_rec, last - cum, NEG_FILL))
        kdec = (k_ref[h].astype(F32) * fade).astype(BF16)
        loc[h, :hd, :] = lax.dot_general(kdec, v_ref[h], TN, preferred_element_type=F32)
        carry = jnp.where(last_rec == before_rec, jnp.exp2(last), 0.0)
        loc[h, hd:, :] = jnp.broadcast_to(carry, (PAD, hd))

    def loc_copy(i):
        h = (1 - half) * half_heads + i
        return send(
            loc.at[h], peer_loc.at[i], loc_send.at[i], loc_recv.at[i], {"ctx": partner}
        )

    loads[2].wait()
    loads[3].wait()
    project(wk_ref.at[0], k_ref, (1 - half) * half_heads)
    loads[4].wait()
    project(wv_ref.at[0], v_ref, (1 - half) * half_heads)
    pl.semaphore_wait(barrier, n - 1 + dp_n - 1)

    @pl.when(pair == 0)
    def _():
        chain_in[...] = jnp.zeros_like(chain_in)

    for i in range(half_heads):
        local_state((1 - half) * half_heads + i)
        loc_copy(i).start()
    loads[5].wait()
    project(wk_ref.at[1], k_ref, half * half_heads)
    loads[6].wait()
    project(wv_ref.at[1], v_ref, half * half_heads)
    for i in range(half_heads):
        local_state(half * half_heads + i)

    def chain_copy(i):
        return send(
            chain_out.at[i],
            chain_in.at[i],
            chain_send.at[i],
            chain_recv.at[i],
            {"ctx": lax.rem(me + 2, n)},
        )

    def hand_copy(i):
        return send(
            hand.at[i],
            state.at[half * half_heads + i],
            hand_send.at[i],
            hand_recv.at[i],
            {"ctx": partner},
        )

    def hand_arrival(i):
        return send(
            hand.at[i],
            state.at[(1 - half) * half_heads + i],
            hand_send.at[i],
            hand_recv.at[i],
            {"ctx": partner},
        )

    def chain_step(i):
        h = half * half_heads + i
        loc_copy(i).wait_recv()

        @pl.when(pair > 0)
        def _():
            chain_copy(i).wait_recv()

        came = chain_in[i]
        own = loc[h]
        other = peer_loc[i]
        first = jnp.where(even, own, other)
        second = jnp.where(even, other, own)
        middle = first[hd : hd + 1, :] * came + first[:hd, :]

        @pl.when(pair < pairs - 1)
        def _():
            chain_out[i] = second[hd : hd + 1, :] * middle + second[:hd, :]
            chain_copy(i).start()

        hand[i] = jnp.where(even, middle, came)
        hand_copy(i).start()
        state[h] = jnp.where(even, came, middle)

    group = 2
    units = heads + heads // group
    first_unit = jnp.minimum(1 + (7 * pair) // 2, units)

    def maybe_chain(unit):
        i = unit - first_unit

        @pl.when((i >= 0) & (i < half_heads))
        def _():
            chain_step(i)

    loads[7].wait()
    project(wq_ref, q_ref, 0)
    loads[8].wait()

    chunk = min(256, labels)

    def pool_unit(h):
        lanes = pl.ds(pl.multiple_of(h * hd, hd), hd)
        rec = col_record(chunk)
        for c in range(labels // chunk):
            cols = slice(c * chunk, (c + 1) * chunk)
            scores = lax.dot_general(
                x_ref[:, lanes], lq_ref[cols, lanes], NT, preferred_element_type=F32
            )
            tops = [
                jnp.max(jnp.where(rec == r, scores, NEG_FILL), axis=0, keepdims=True)
                for r in range(recs)
            ]
            top = tops[0]
            for r in range(1, recs):
                top = jnp.where(rec == r, tops[r], top)
            weight = jnp.exp2((scores - top) * soft)
            pool_w[h, :, cols] = weight
            for r in range(recs):
                stats[h, r : r + 1, cols] = tops[r] * soft
                stats[h, recs + r : recs + r + 1, cols] = jnp.sum(
                    jnp.where(rec == r, weight, 0.0), axis=0, keepdims=True
                )

    def pool_body(h, _):
        pool_unit(h)
        maybe_chain(h)
        return 0

    lax.fori_loop(0, heads, pool_body, 0)

    def stat_copy(d):
        target = lax.rem(me + d, n)
        return target, send(
            stats.at[lax.rem(target, heads)],
            stat_in.at[me],
            stat_send.at[d],
            stat_recv.at[d],
            {"ctx": target},
        )

    def stat_arrival(d):
        return send(
            stats.at[0],
            stat_in.at[lax.rem(me - d + n, n)],
            stat_send.at[d],
            stat_recv.at[d],
            {"ctx": lax.rem(me + d, n)},
        )

    def each_peer(fn):
        for d in range(1, n):
            fn(d)

    def start_stat(d):
        target, copy = stat_copy(d)

        @pl.when(target < heads)
        def _():
            copy.start()

    each_peer(start_stat)

    def intra_unit(h):
        scores = lax.dot_general(q_ref[h], k_ref[h], NT, preferred_element_type=F32)
        cum = jnp.concatenate([ccol[h]] * (tok // hd), axis=1)
        fade = jnp.exp2(cum - crow[h] + pair_bias[...])
        weights = (scores * fade).astype(BF16)
        intra[h] = jnp.dot(weights, v_ref[h], preferred_element_type=F32)

    def intra_body(u, _):
        for s in range(group):
            intra_unit(u * group + s)
        maybe_chain(heads + u)
        return 0

    lax.fori_loop(0, heads // group, intra_body, 0)

    def lse_copy(d):
        return send(
            lse.at[lax.rem(me, heads)],
            lse.at[lax.rem(me, heads)],
            lse_send.at[d],
            lse_recv.at[d],
            {"ctx": lax.rem(me + d, n)},
        )

    def lse_arrival(d):
        source = lax.rem(me - d + n, n)
        return source, send(
            lse.at[lax.rem(source, heads)],
            lse.at[lax.rem(source, heads)],
            lse_send.at[d],
            lse_recv.at[d],
            {"ctx": lax.rem(me + d, n)},
        )

    @pl.when(me < heads)
    def _():
        stat_in[me] = stats[lax.rem(me, heads)]
        each_peer(lambda d: stat_arrival(d).wait_recv())
        top = stat_in[0, :recs, :]
        for j in range(1, n):
            top = jnp.maximum(top, stat_in[j, :recs, :])
        mass = jnp.zeros_like(top)
        for j in range(n):
            mass = mass + stat_in[j, recs:, :] * jnp.exp2(stat_in[j, :recs, :] - top)
        lse[lax.rem(me, heads)] = top + jnp.log(mass) * LOG2E
        each_peer(lambda d: lse_copy(d).start())

    loads[10].wait()
    hot = (
        lax.broadcasted_iota(jnp.int32, (labels, tok), 0) == label_ref[...]
    ).astype(F32).astype(BF16)
    members = (
        row_record(16) == lax.broadcasted_iota(jnp.int32, (16, tok), 0)
    ).astype(F32).astype(BF16)
    counts = lax.dot_general(members, hot, NT, preferred_element_type=F32)
    contrib[recs:, :] = counts[:recs, :]

    loads[9].wait()
    loads[11].wait()

    def finish(h):
        lanes = pl.ds(pl.multiple_of(h * hd, hd), hd)
        st = state[h]
        high = st.astype(BF16)
        low = (st - high.astype(F32)).astype(BF16)
        q = q_ref[h]
        inter = jnp.dot(
            jnp.concatenate([q, q], axis=1),
            jnp.concatenate([high, low], axis=0),
            preferred_element_type=F32,
        )
        fade = jnp.exp2(
            jnp.where(col_record(hd) == before_rec, ccol[h] + math.log2(scale), NEG_FILL)
        )
        total = intra[h] + inter * fade
        centred = total - jnp.mean(total, axis=1, keepdims=True)
        variance = jnp.mean(centred * centred, axis=1, keepdims=True)
        rows = (centred * lax.rsqrt(variance + 1e-05) * gain_ref[pl.ds(h, 1), :]).astype(BF16)
        out_buf[:, lanes] = rows
        rec = col_record(chunk)
        for c in range(labels // chunk):
            cols = slice(c * chunk, (c + 1) * chunk)
            value = lax.dot_general(rows, lw_ref[cols, lanes], NT, preferred_element_type=F32)
            value = value * pool_w[h, :, cols]
            for r in range(recs):
                weighted[h, r : r + 1, cols] = jnp.sum(
                    jnp.where(rec == r, value, 0.0), axis=0, keepdims=True
                )

    for i in range(half_heads + 1):
        if i < half_heads:

            @pl.when(first_unit + i >= units)
            def _():
                chain_step(i)

        if i > 0:
            hand_arrival(i - 1).wait_recv()
        if i < half_heads:
            finish(half * half_heads + i)
        if i > 0:
            finish((1 - half) * half_heads + i - 1)

    store = pltpu.make_async_copy(out_buf, out_hbm, out_sem)
    store.start()

    def wait_lse(d):
        source, copy = lse_arrival(d)

        @pl.when(source < heads)
        def _():
            copy.wait_recv()

    each_peer(wait_lse)
    part = jnp.zeros((recs, labels), F32)
    for h in range(heads):
        part = part + weighted[h] * jnp.exp2(stats[h, :recs, :] - lse[h])
    contrib[:recs, :] = part

    def con_copy(d):
        return send(
            contrib,
            contrib_in.at[d],
            con_send.at[d],
            con_recv.at[d],
            {"ctx": lax.rem(me + d, n)},
        )

    each_peer(lambda d: con_copy(d).start())
    contrib_in[0] = contrib[...]
    each_peer(lambda d: con_copy(d).wait_recv())
    both = contrib_in[lax.rem(me, n)]
    for j in range(1, n):
        both = both + contrib_in[lax.rem(me - j + n, n)]
    logits = both[:recs, :]
    logits_ref[...] = logits
    losses = []
    total_loss = jnp.zeros((1, 1), F32)
    for r in range(recs):
        z = logits[r : r + 1, :]
        target = (both[recs + r : recs + r + 1, :] + 0.5) / (
            lengths_ref[0, r].astype(F32) + 1.0
        )
        soft_plus = jnp.maximum(z, 0.0) + jnp.log1p(jnp.exp(-jnp.abs(z)))
        value = jnp.mean(soft_plus - target * z, axis=1, keepdims=True)
        losses.append(value)
        total_loss = total_loss + value
    spot = lax.broadcasted_iota(jnp.int32, (1, recs), 1)
    row = jnp.zeros((1, recs), F32)
    for r in range(recs):
        row = jnp.where(spot == r, losses[r], row)
    loss_ref[...] = row
    loss_out[...] = jnp.broadcast_to(total_loss, loss_out.shape)

    def dp_copy(d):
        return send(
            loss_out,
            loss_in.at[d],
            dp_send.at[d],
            dp_recv.at[d],
            {"dp": lax.rem(my_dp + d, dp_n)},
        )

    for d in range(1, dp_n):
        dp_copy(d).start()
    loss_in[0] = loss_out[...]
    for d in range(1, dp_n):
        dp_copy(d).wait_recv()
    total = loss_in[lax.rem(my_dp, dp_n)]
    for j in range(1, dp_n):
        total = total + loss_in[lax.rem(my_dp - j + dp_n, dp_n)]
    mean_ref[...] = total[:1, :1] / (dp_n * recs)

    for d in range(1, dp_n):
        dp_copy(d).wait_send()
    each_peer(lambda d: con_copy(d).wait_send())

    @pl.when(me < heads)
    def _():
        each_peer(lambda d: lse_copy(d).wait_send())

    def end_stat(d):
        target, copy = stat_copy(d)

        @pl.when(target < heads)
        def _():
            copy.wait_send()

    each_peer(end_stat)
    for i in range(half_heads):
        loc_copy(i).wait_send()
        hand_copy(i).wait_send()

    @pl.when(pair < pairs - 1)
    def _():
        for i in range(half_heads):
            chain_copy(i).wait_send()

    store.wait()


def write_out(*refs):
    sems = refs[8]
    copies = [pltpu.make_async_copy(refs[i], refs[4 + i], sems.at[i]) for i in range(4)]
    for copy in copies:
        copy.start()
    for copy in copies:
        copy.wait()


def local(
    tokens,
    log_decay,
    lengths,
    label_ids,
    w_query,
    w_key,
    w_value,
    norm_gain,
    label_query,
    label_weight,
):
    n = lax.axis_size("ctx")
    dp_n = lax.axis_size("dp")
    tok, width = tokens.shape[1:]
    heads = log_decay.shape[1]
    hd = width // heads
    recs = lengths.shape[1]
    labels = label_query.shape[0]
    half = heads // 2
    assert n >= heads and n % 2 == 0
    any_space = pl.BlockSpec(memory_space=pl.ANY)
    hbm = pl.BlockSpec(memory_space=pltpu.HBM)
    vmem = pl.BlockSpec(memory_space=pltpu.VMEM)
    dma = pltpu.SemaphoreType.DMA
    out_shape = (
        jax.ShapeDtypeStruct((tok, width), BF16),
        jax.ShapeDtypeStruct((recs, labels), F32),
        jax.ShapeDtypeStruct((1, recs), F32),
        jax.ShapeDtypeStruct((1, 1), F32),
    )
    results = pl.pallas_call(
        functools.partial(fused, n, dp_n),
        out_shape=out_shape,
        in_specs=[hbm] * 10,
        out_specs=(hbm,) + (vmem,) * 3,
        scratch_shapes=[
            pltpu.SMEM((1, recs), jnp.int32),
            pltpu.VMEM((heads, tok), F32),
            pltpu.VMEM((1, tok), jnp.int32),
            pltpu.VMEM((heads, hd), F32),
            pltpu.VMEM((tok, width), BF16),
            pltpu.VMEM((width, width), BF16),
            pltpu.VMEM((2, width, width // 2), BF16),
            pltpu.VMEM((2, width, width // 2), BF16),
            pltpu.VMEM((labels, width), BF16),
            pltpu.VMEM((labels, width), BF16),
            pltpu.VMEM((heads, tok, hd), BF16),
            pltpu.VMEM((heads, tok, hd), BF16),
            pltpu.VMEM((heads, tok, hd), BF16),
            pltpu.VMEM((heads, tok, hd), F32),
            pltpu.VMEM((heads, 1, tok), F32),
            pltpu.VMEM((tok, tok), F32),
            pltpu.VMEM((heads, tok, hd), F32),
            pltpu.VMEM((heads, tok, labels), F32),
            pltpu.VMEM((heads, recs, labels), F32),
            pltpu.VMEM((tok, width), BF16),
            pltpu.VMEM((heads, hd + PAD, hd), F32),
            pltpu.VMEM((half, hd + PAD, hd), F32),
            pltpu.VMEM((half, hd, hd), F32),
            pltpu.VMEM((half, hd, hd), F32),
            pltpu.VMEM((half, hd, hd), F32),
            pltpu.VMEM((heads, hd, hd), F32),
            pltpu.VMEM((heads, 2 * recs, labels), F32),
            pltpu.VMEM((n, 2 * recs, labels), F32),
            pltpu.VMEM((heads, recs, labels), F32),
            pltpu.VMEM((2 * recs, labels), F32),
            pltpu.VMEM((n, 2 * recs, labels), F32),
            pltpu.VMEM((8, 128), F32),
            pltpu.VMEM((dp_n, 8, 128), F32),
            dma((12,)),
            dma,
            dma((half,)),
            dma((half,)),
            dma((half,)),
            dma((half,)),
            dma((half,)),
            dma((half,)),
            dma((n,)),
            dma((n,)),
            dma((n,)),
            dma((n,)),
            dma((n,)),
            dma((n,)),
            dma((dp_n,)),
            dma((dp_n,)),
        ],
        compiler_params=pltpu.CompilerParams(
            collective_id=0, has_side_effects=True, vmem_limit_bytes=VMEM_LIMIT
        ),
    )(
        lengths,
        log_decay[0],
        label_ids,
        norm_gain.reshape(heads, hd),
        tokens[0],
        w_query,
        w_key,
        w_value,
        label_query,
        label_weight,
    )
    out, logits, loss, mean = pl.pallas_call(
        write_out,
        out_shape=out_shape,
        in_specs=[any_space] * 4,
        out_specs=(hbm,) * 4,
        scratch_shapes=[dma((4,))],
        compiler_params=pltpu.CompilerParams(vmem_limit_bytes=VMEM_LIMIT),
    )(*results)
    return (out[None], logits[None], loss, mean.reshape(()))


def solution(mesh):
    return jax.shard_map(
        local,
        mesh=mesh,
        in_specs=(
            P("dp", "ctx", None),
            P("dp", None, "ctx"),
            P("dp", None),
            P("dp", "ctx"),
            P(),
            P(),
            P(),
            P(),
            P(),
            P(),
        ),
        out_specs=(P("dp", "ctx", None), P("dp", None, None), P("dp", None), P()),
        check_vma=False,
    )
```

```python
import functools
import math

import jax
import jax.numpy as jnp
from jax import lax
from jax.experimental import pallas as pl
from jax.experimental.pallas import tpu as pltpu
from jax.sharding import PartitionSpec as P

NEG_FILL = -1e30
LOG2E = math.log2(math.e)
F32 = jnp.float32
BF16 = jnp.bfloat16
NT = (((1,), (1,)), ((), ()))
TN = (((0,), (0,)), ((), ()))
PAD = 8
PIECES = 2
VMEM_LIMIT = 63 * 1024 * 1024


def fused(
    n,
    dp_n,
    lengths_hbm,
    decay_hbm,
    label_hbm,
    gain_hbm,
    tokens_hbm,
    wq_hbm,
    wk_hbm,
    wv_hbm,
    lq_hbm,
    lw_hbm,
    out_hbm,
    logits_ref,
    loss_ref,
    mean_ref,
    lengths_ref,
    decay_ref,
    label_ref,
    gain_ref,
    x_ref,
    wq_ref,
    wk_ref,
    wv_ref,
    lq_ref,
    lw_ref,
    q_ref,
    k_ref,
    v_ref,
    ccol,
    crow,
    pair_bias,
    intra,
    pool_w,
    weighted,
    out_buf,
    loc,
    peer_loc,
    chain_in,
    chain_out,
    hand,
    state,
    stats,
    stat_in,
    lse,
    contrib,
    contrib_in,
    loss_out,
    loss_in,
    in_sem,
    out_sem,
    loc_send,
    loc_recv,
    chain_send,
    chain_recv,
    hand_send,
    hand_recv,
    stat_send,
    stat_recv,
    lse_send,
    lse_recv,
    con_send,
    con_recv,
    dp_send,
    dp_recv,
):
    tok, width = x_ref.shape
    heads, _, hd = q_ref.shape
    labels = lq_ref.shape[0]
    recs = lengths_ref.shape[1]
    half_heads = heads // 2
    pairs = n // 2
    scale = hd ** (-0.5)
    soft = scale * LOG2E
    me = lax.axis_index("ctx")
    my_dp = lax.axis_index("dp")
    half = lax.rem(me, 2)
    pair = me // 2
    partner = me + 1 - 2 * half
    even = half == 0

    part = half_heads * hd
    far_cols = pl.ds(pl.multiple_of((1 - half) * part, part), part)
    near_cols = pl.ds(pl.multiple_of(half * part, part), part)
    plan = (
        (lengths_hbm, lengths_ref),
        (decay_hbm, decay_ref),
        (tokens_hbm, x_ref),
        (wk_hbm.at[:, far_cols], wk_ref.at[0]),
        (wv_hbm.at[:, far_cols], wv_ref.at[0]),
        (wk_hbm.at[:, near_cols], wk_ref.at[1]),
        (wv_hbm.at[:, near_cols], wv_ref.at[1]),
        (wq_hbm, wq_ref),
        (lq_hbm, lq_ref),
        (lw_hbm, lw_ref),
        (label_hbm, label_ref),
        (gain_hbm, gain_ref),
    )
    loads = [pltpu.make_async_copy(src, dst, in_sem.at[i]) for i, (src, dst) in enumerate(plan)]
    for load in loads[:5]:
        load.start()

    barrier = pltpu.get_barrier_semaphore()
    for d in range(1, n):
        pl.semaphore_signal(
            barrier,
            inc=1,
            device_id={"ctx": lax.rem(me + d, n)},
            device_id_type=pl.DeviceIdType.MESH,
        )
    for d in range(1, dp_n):
        pl.semaphore_signal(
            barrier,
            inc=1,
            device_id={"dp": lax.rem(my_dp + d, dp_n)},
            device_id_type=pl.DeviceIdType.MESH,
        )

    def send(src, dst, ssem, rsem, where):
        return pltpu.make_async_remote_copy(
            src_ref=src,
            dst_ref=dst,
            send_sem=ssem,
            recv_sem=rsem,
            device_id=where,
            device_id_type=pl.DeviceIdType.MESH,
        )

    loads[0].wait()
    loads[1].wait()
    shard_start = me * tok
    starts = []
    run = jnp.int32(0)
    for r in range(recs):
        starts.append(run)
        run = run + lengths_ref[0, r]

    def record_of(pos):
        rec = jnp.full_like(pos, -1)
        for r in range(recs):
            rec = rec + (starts[r] <= pos).astype(jnp.int32)
        return rec

    def record_scalar(pos):
        rec = jnp.int32(-1)
        for r in range(recs):
            rec = rec + (starts[r] <= pos).astype(jnp.int32)
        return rec

    before_rec = record_scalar(shard_start - 1)
    last_rec = record_scalar(shard_start + tok - 1)

    def col_record(lanes):
        return record_of(shard_start + lax.broadcasted_iota(jnp.int32, (tok, lanes), 0))

    def row_record(rows):
        return record_of(shard_start + lax.broadcasted_iota(jnp.int32, (rows, tok), 1))

    down = lax.broadcasted_iota(jnp.int32, (tok, tok), 0)
    across = lax.broadcasted_iota(jnp.int32, (tok, tok), 1)
    tri_low = (across <= down).astype(F32)
    decays = decay_ref[...]
    cum_rows = (
        lax.dot_general(
            decays, tri_low, NT, precision=lax.Precision.HIGHEST, preferred_element_type=F32
        )
        * LOG2E
    )
    cum_cols = (
        lax.dot_general(
            tri_low, decays, NT, precision=lax.Precision.HIGHEST, preferred_element_type=F32
        )
        * LOG2E
    )
    for h in range(heads):
        crow[h] = cum_rows[h : h + 1, :]
        ccol[h] = jnp.broadcast_to(cum_cols[:, h : h + 1], (tok, hd))
    pair_ok = (across <= down) & (col_record(tok) == row_record(tok))
    pair_bias[...] = jnp.where(pair_ok, math.log2(scale), NEG_FILL)

    def project(w_ref, dst, first):
        columns = w_ref.shape[1]
        step = min(256, columns)
        for c in range(columns // step):
            res = jnp.dot(
                x_ref[...], w_ref[:, c * step : (c + 1) * step], preferred_element_type=F32
            ).astype(BF16)
            for s in range(step // hd):
                dst[first + c * (step // hd) + s] = res[:, s * hd : (s + 1) * hd]

    piece = hd // PIECES

    def local_state(h):
        cum = ccol[h]
        last = cum[tok - 1 : tok, :]
        fade = jnp.exp2(jnp.where(col_record(hd) == last_rec, last - cum, NEG_FILL))
        kdec = (k_ref[h].astype(F32) * fade).astype(BF16)
        made = lax.dot_general(kdec, v_ref[h], TN, preferred_element_type=F32)
        carry = jnp.where(last_rec == before_rec, jnp.exp2(last), 0.0)
        for s in range(PIECES):
            loc[h, s, :piece, :] = made[s * piece : (s + 1) * piece, :]
            loc[h, s, piece:, :] = jnp.broadcast_to(carry, (PAD, hd))

    def loc_copy(i, s):
        h = (1 - half) * half_heads + i
        return send(
            loc.at[h, s],
            peer_loc.at[i, s],
            loc_send.at[i, s],
            loc_recv.at[i, s],
            {"ctx": partner},
        )

    loads[2].wait()
    loads[3].wait()
    for load in loads[5:7]:
        load.start()
    project(wk_ref.at[0], k_ref, (1 - half) * half_heads)
    loads[4].wait()
    for load in loads[7:]:
        load.start()
    project(wv_ref.at[0], v_ref, (1 - half) * half_heads)
    pl.semaphore_wait(barrier, n - 1 + dp_n - 1)

    @pl.when(pair == 0)
    def _():
        chain_in[...] = jnp.zeros_like(chain_in)

    for i in range(half_heads):
        local_state((1 - half) * half_heads + i)
        for s in range(PIECES):
            loc_copy(i, s).start()
    def chain_copy(i, s):
        return send(
            chain_out.at[i, s],
            chain_in.at[i, s],
            chain_send.at[i, s],
            chain_recv.at[i, s],
            {"ctx": lax.rem(me + 2, n)},
        )

    def hand_to(i, s, h):
        return send(
            hand.at[i, s],
            state.at[h, s],
            hand_send.at[i, s],
            hand_recv.at[i, s],
            {"ctx": partner},
        )

    def hand_copy(i, s):
        return hand_to(i, s, half * half_heads + i)

    def hand_arrival(i, s):
        return hand_to(i, s, (1 - half) * half_heads + i)

    def chain_step(i):
        h = half * half_heads + i
        for s in range(PIECES):
            loc_copy(i, s).wait_recv()

            @pl.when(pair > 0)
            def _():
                chain_copy(i, s).wait_recv()

            came = chain_in[i, s]
            own = loc[h, s]
            other = peer_loc[i, s]
            first = jnp.where(even, own, other)
            second = jnp.where(even, other, own)
            middle = first[piece : piece + 1, :] * came + first[:piece, :]

            @pl.when(pair < pairs - 1)
            def _():
                chain_out[i, s] = second[piece : piece + 1, :] * middle + second[:piece, :]
                chain_copy(i, s).start()

            hand[i, s] = jnp.where(even, middle, came)
            hand_copy(i, s).start()
            state[h, s] = jnp.where(even, came, middle)

    loads[5].wait()
    project(wk_ref.at[1], k_ref, half * half_heads)
    loads[6].wait()
    project(wv_ref.at[1], v_ref, half * half_heads)
    for i in range(half_heads):
        local_state(half * half_heads + i)

        @pl.when(pair == 0)
        def _():
            chain_step(i)

    group = 2
    units = heads + heads // group
    first_unit = jnp.where(pair == 0, -half_heads, jnp.minimum(4 * pair - 3, units))

    def maybe_chain(unit):
        i = unit - first_unit

        @pl.when((i >= 0) & (i < half_heads))
        def _():
            chain_step(i)

    loads[7].wait()
    project(wq_ref, q_ref, 0)
    loads[8].wait()

    chunk = min(256, labels)

    def pool_unit(h):
        lanes = pl.ds(pl.multiple_of(h * hd, hd), hd)
        rec = col_record(chunk)
        for c in range(labels // chunk):
            cols = slice(c * chunk, (c + 1) * chunk)
            scores = lax.dot_general(
                x_ref[:, lanes], lq_ref[cols, lanes], NT, preferred_element_type=F32
            )
            tops = [
                jnp.max(jnp.where(rec == r, scores, NEG_FILL), axis=0, keepdims=True)
                for r in range(recs)
            ]
            top = tops[0]
            for r in range(1, recs):
                top = jnp.where(rec == r, tops[r], top)
            weight = jnp.exp2((scores - top) * soft)
            pool_w[h, :, cols] = weight
            for r in range(recs):
                stats[h, r : r + 1, cols] = tops[r] * soft
                stats[h, recs + r : recs + r + 1, cols] = jnp.sum(
                    jnp.where(rec == r, weight, 0.0), axis=0, keepdims=True
                )

    def pool_body(h, _):
        pool_unit(h)
        maybe_chain(h)
        return 0

    lax.fori_loop(0, heads, pool_body, 0)

    def stat_copy(d):
        target = lax.rem(me + d, n)
        return target, send(
            stats.at[lax.rem(target, heads)],
            stat_in.at[me],
            stat_send.at[d],
            stat_recv.at[d],
            {"ctx": target},
        )

    def stat_arrival(d):
        return send(
            stats.at[0],
            stat_in.at[lax.rem(me - d + n, n)],
            stat_send.at[d],
            stat_recv.at[d],
            {"ctx": lax.rem(me + d, n)},
        )

    def each_peer(fn):
        for d in range(1, n):
            fn(d)

    def start_stat(d):
        target, copy = stat_copy(d)

        @pl.when(target < heads)
        def _():
            copy.start()

    each_peer(start_stat)

    def intra_unit(h):
        scores = lax.dot_general(q_ref[h], k_ref[h], NT, preferred_element_type=F32)
        cum = jnp.concatenate([ccol[h]] * (tok // hd), axis=1)
        fade = jnp.exp2(cum - crow[h] + pair_bias[...])
        weights = (scores * fade).astype(BF16)
        intra[h] = jnp.dot(weights, v_ref[h], preferred_element_type=F32)

    def intra_body(u, _):
        for s in range(group):
            intra_unit(u * group + s)
        maybe_chain(heads + u)
        return 0

    lax.fori_loop(0, heads // group, intra_body, 0)

    def lse_copy(d):
        return send(
            lse.at[lax.rem(me, heads)],
            lse.at[lax.rem(me, heads)],
            lse_send.at[d],
            lse_recv.at[d],
            {"ctx": lax.rem(me + d, n)},
        )

    def lse_arrival(d):
        source = lax.rem(me - d + n, n)
        return source, send(
            lse.at[lax.rem(source, heads)],
            lse.at[lax.rem(source, heads)],
            lse_send.at[d],
            lse_recv.at[d],
            {"ctx": lax.rem(me + d, n)},
        )

    @pl.when(me < heads)
    def _():
        stat_in[me] = stats[lax.rem(me, heads)]
        each_peer(lambda d: stat_arrival(d).wait_recv())
        top = stat_in[0, :recs, :]
        for j in range(1, n):
            top = jnp.maximum(top, stat_in[j, :recs, :])
        mass = jnp.zeros_like(top)
        for j in range(n):
            mass = mass + stat_in[j, recs:, :] * jnp.exp2(stat_in[j, :recs, :] - top)
        lse[lax.rem(me, heads)] = top + jnp.log(mass) * LOG2E
        each_peer(lambda d: lse_copy(d).start())

    loads[10].wait()
    hot = (
        lax.broadcasted_iota(jnp.int32, (labels, tok), 0) == label_ref[...]
    ).astype(F32).astype(BF16)
    members = (
        row_record(16) == lax.broadcasted_iota(jnp.int32, (16, tok), 0)
    ).astype(F32).astype(BF16)
    counts = lax.dot_general(members, hot, NT, preferred_element_type=F32)
    contrib[recs:, :] = counts[:recs, :]

    loads[9].wait()
    loads[11].wait()

    def finish(h):
        lanes = pl.ds(pl.multiple_of(h * hd, hd), hd)
        st = jnp.concatenate([state[h, s] for s in range(PIECES)], axis=0)
        high = st.astype(BF16)
        low = (st - high.astype(F32)).astype(BF16)
        q = q_ref[h]
        inter = jnp.dot(
            jnp.concatenate([q, q], axis=1),
            jnp.concatenate([high, low], axis=0),
            preferred_element_type=F32,
        )
        fade = jnp.exp2(
            jnp.where(col_record(hd) == before_rec, ccol[h] + math.log2(scale), NEG_FILL)
        )
        total = intra[h] + inter * fade
        centred = total - jnp.mean(total, axis=1, keepdims=True)
        variance = jnp.mean(centred * centred, axis=1, keepdims=True)
        rows = (centred * lax.rsqrt(variance + 1e-05) * gain_ref[pl.ds(h, 1), :]).astype(BF16)
        out_buf[:, lanes] = rows
        rec = col_record(chunk)
        for c in range(labels // chunk):
            cols = slice(c * chunk, (c + 1) * chunk)
            value = lax.dot_general(rows, lw_ref[cols, lanes], NT, preferred_element_type=F32)
            value = value * pool_w[h, :, cols]
            for r in range(recs):
                weighted[h, r : r + 1, cols] = jnp.sum(
                    jnp.where(rec == r, value, 0.0), axis=0, keepdims=True
                )

    for i in range(half_heads + 1):
        if i < half_heads:

            @pl.when(first_unit + i >= units)
            def _():
                chain_step(i)

        if i > 0:
            for s in range(PIECES):
                hand_arrival(i - 1, s).wait_recv()
        if i < half_heads:
            finish(half * half_heads + i)
        if i > 0:
            finish((1 - half) * half_heads + i - 1)

    store = pltpu.make_async_copy(out_buf, out_hbm, out_sem)
    store.start()

    def wait_lse(d):
        source, copy = lse_arrival(d)

        @pl.when(source < heads)
        def _():
            copy.wait_recv()

    each_peer(wait_lse)
    part = jnp.zeros((recs, labels), F32)
    for h in range(heads):
        part = part + weighted[h] * jnp.exp2(stats[h, :recs, :] - lse[h])
    contrib[:recs, :] = part

    def con_copy(d):
        return send(
            contrib,
            contrib_in.at[d],
            con_send.at[d],
            con_recv.at[d],
            {"ctx": lax.rem(me + d, n)},
        )

    each_peer(lambda d: con_copy(d).start())
    contrib_in[0] = contrib[...]
    each_peer(lambda d: con_copy(d).wait_recv())
    both = contrib_in[lax.rem(me, n)]
    for j in range(1, n):
        both = both + contrib_in[lax.rem(me - j + n, n)]
    logits = both[:recs, :]
    logits_ref[...] = logits
    losses = []
    total_loss = jnp.zeros((1, 1), F32)
    for r in range(recs):
        z = logits[r : r + 1, :]
        target = (both[recs + r : recs + r + 1, :] + 0.5) / (
            lengths_ref[0, r].astype(F32) + 1.0
        )
        soft_plus = jnp.maximum(z, 0.0) + jnp.log1p(jnp.exp(-jnp.abs(z)))
        value = jnp.mean(soft_plus - target * z, axis=1, keepdims=True)
        losses.append(value)
        total_loss = total_loss + value
    spot = lax.broadcasted_iota(jnp.int32, (1, recs), 1)
    row = jnp.zeros((1, recs), F32)
    for r in range(recs):
        row = jnp.where(spot == r, losses[r], row)
    loss_ref[...] = row
    loss_out[...] = jnp.broadcast_to(total_loss, loss_out.shape)

    def dp_copy(d):
        return send(
            loss_out,
            loss_in.at[d],
            dp_send.at[d],
            dp_recv.at[d],
            {"dp": lax.rem(my_dp + d, dp_n)},
        )

    for d in range(1, dp_n):
        dp_copy(d).start()
    loss_in[0] = loss_out[...]
    for d in range(1, dp_n):
        dp_copy(d).wait_recv()
    total = loss_in[lax.rem(my_dp, dp_n)]
    for j in range(1, dp_n):
        total = total + loss_in[lax.rem(my_dp - j + dp_n, dp_n)]
    mean_ref[...] = total[:1, :1] / (dp_n * recs)

    for d in range(1, dp_n):
        dp_copy(d).wait_send()
    each_peer(lambda d: con_copy(d).wait_send())

    @pl.when(me < heads)
    def _():
        each_peer(lambda d: lse_copy(d).wait_send())

    def end_stat(d):
        target, copy = stat_copy(d)

        @pl.when(target < heads)
        def _():
            copy.wait_send()

    each_peer(end_stat)
    for i in range(half_heads):
        for s in range(PIECES):
            loc_copy(i, s).wait_send()
            hand_copy(i, s).wait_send()

    @pl.when(pair < pairs - 1)
    def _():
        for i in range(half_heads):
            for s in range(PIECES):
                chain_copy(i, s).wait_send()

    store.wait()


def write_out(*refs):
    ins, outs, held, sems = refs[:4], refs[4:8], refs[8:12], refs[12]
    rows = ins[0].shape[0] // 2
    pieces = [(i, ins[i], outs[i], held[i]) for i in range(1, 4)]
    for p in range(2):
        cut = pl.ds(p * rows, rows)
        pieces.append((4 * p, ins[0].at[cut], outs[0].at[cut], held[0].at[cut]))
    fetches = [pltpu.make_async_copy(src, mid, sems.at[0, i]) for i, src, dst, mid in pieces]
    stores = [pltpu.make_async_copy(mid, dst, sems.at[1, i]) for i, src, dst, mid in pieces]
    for fetch in fetches:
        fetch.start()
    for fetch, store in zip(fetches, stores):
        fetch.wait()
        store.start()
    for store in stores:
        store.wait()


def local(
    tokens,
    log_decay,
    lengths,
    label_ids,
    w_query,
    w_key,
    w_value,
    norm_gain,
    label_query,
    label_weight,
):
    n = lax.axis_size("ctx")
    dp_n = lax.axis_size("dp")
    tok, width = tokens.shape[1:]
    heads = log_decay.shape[1]
    hd = width // heads
    recs = lengths.shape[1]
    labels = label_query.shape[0]
    half = heads // 2
    piece = hd // PIECES
    assert n >= heads and n % 2 == 0
    any_space = pl.BlockSpec(memory_space=pl.ANY)
    hbm = pl.BlockSpec(memory_space=pltpu.HBM)
    vmem = pl.BlockSpec(memory_space=pltpu.VMEM)
    dma = pltpu.SemaphoreType.DMA
    out_shape = (
        jax.ShapeDtypeStruct((tok, width), BF16),
        jax.ShapeDtypeStruct((recs, labels), F32),
        jax.ShapeDtypeStruct((1, recs), F32),
        jax.ShapeDtypeStruct((1, 1), F32),
    )
    results = pl.pallas_call(
        functools.partial(fused, n, dp_n),
        out_shape=out_shape,
        in_specs=[hbm] * 10,
        out_specs=(hbm,) + (vmem,) * 3,
        scratch_shapes=[
            pltpu.SMEM((1, recs), jnp.int32),
            pltpu.VMEM((heads, tok), F32),
            pltpu.VMEM((1, tok), jnp.int32),
            pltpu.VMEM((heads, hd), F32),
            pltpu.VMEM((tok, width), BF16),
            pltpu.VMEM((width, width), BF16),
            pltpu.VMEM((2, width, width // 2), BF16),
            pltpu.VMEM((2, width, width // 2), BF16),
            pltpu.VMEM((labels, width), BF16),
            pltpu.VMEM((labels, width), BF16),
            pltpu.VMEM((heads, tok, hd), BF16),
            pltpu.VMEM((heads, tok, hd), BF16),
            pltpu.VMEM((heads, tok, hd), BF16),
            pltpu.VMEM((heads, tok, hd), F32),
            pltpu.VMEM((heads, 1, tok), F32),
            pltpu.VMEM((tok, tok), F32),
            pltpu.VMEM((heads, tok, hd), F32),
            pltpu.VMEM((heads, tok, labels), F32),
            pltpu.VMEM((heads, recs, labels), F32),
            pltpu.VMEM((tok, width), BF16),
            pltpu.VMEM((heads, PIECES, piece + PAD, hd), F32),
            pltpu.VMEM((half, PIECES, piece + PAD, hd), F32),
            pltpu.VMEM((half, PIECES, piece, hd), F32),
            pltpu.VMEM((half, PIECES, piece, hd), F32),
            pltpu.VMEM((half, PIECES, piece, hd), F32),
            pltpu.VMEM((heads, PIECES, piece, hd), F32),
            pltpu.VMEM((heads, 2 * recs, labels), F32),
            pltpu.VMEM((n, 2 * recs, labels), F32),
            pltpu.VMEM((heads, recs, labels), F32),
            pltpu.VMEM((2 * recs, labels), F32),
            pltpu.VMEM((n, 2 * recs, labels), F32),
            pltpu.VMEM((8, 128), F32),
            pltpu.VMEM((dp_n, 8, 128), F32),
            dma((12,)),
            dma,
            dma((half, PIECES)),
            dma((half, PIECES)),
            dma((half, PIECES)),
            dma((half, PIECES)),
            dma((half, PIECES)),
            dma((half, PIECES)),
            dma((n,)),
            dma((n,)),
            dma((n,)),
            dma((n,)),
            dma((n,)),
            dma((n,)),
            dma((dp_n,)),
            dma((dp_n,)),
        ],
        compiler_params=pltpu.CompilerParams(
            collective_id=0, has_side_effects=True, vmem_limit_bytes=VMEM_LIMIT
        ),
    )(
        lengths,
        log_decay[0],
        label_ids,
        norm_gain.reshape(heads, hd),
        tokens[0],
        w_query,
        w_key,
        w_value,
        label_query,
        label_weight,
    )
    out, logits, loss, mean = pl.pallas_call(
        write_out,
        out_shape=out_shape,
        in_specs=[any_space] * 4,
        out_specs=(hbm,) * 4,
        scratch_shapes=[pltpu.VMEM(o.shape, o.dtype) for o in out_shape] + [dma((2, 5))],
        compiler_params=pltpu.CompilerParams(vmem_limit_bytes=VMEM_LIMIT),
    )(*results)
    return (out[None], logits[None], loss, mean.reshape(()))


def solution(mesh):
    return jax.shard_map(
        local,
        mesh=mesh,
        in_specs=(
            P("dp", "ctx", None),
            P("dp", None, "ctx"),
            P("dp", None),
            P("dp", "ctx"),
            P(),
            P(),
            P(),
            P(),
            P(),
            P(),
        ),
        out_specs=(P("dp", "ctx", None), P("dp", None, None), P("dp", None), P()),
        check_vma=False,
    )
```

```python
import functools
import math

import jax
import jax.numpy as jnp
from jax import lax
from jax.experimental import pallas as pl
from jax.experimental.pallas import tpu as pltpu
from jax.sharding import PartitionSpec as P

NEG_FILL = -1e30
LOG2E = math.log2(math.e)
F32 = jnp.float32
BF16 = jnp.bfloat16
NT = (((1,), (1,)), ((), ()))
TN = (((0,), (0,)), ((), ()))
PAD = 8
PIECES = 2
VMEM_LIMIT = 63 * 1024 * 1024


def fused(
    n,
    dp_n,
    lengths_hbm,
    decay_hbm,
    label_hbm,
    gain_hbm,
    tokens_hbm,
    wq_hbm,
    wk_hbm,
    wv_hbm,
    lq_hbm,
    lw_hbm,
    out_hbm,
    logits_ref,
    loss_ref,
    mean_ref,
    lengths_ref,
    decay_ref,
    label_ref,
    gain_ref,
    x_ref,
    wq_ref,
    wk_ref,
    wv_ref,
    lq_ref,
    lw_ref,
    q_ref,
    k_ref,
    v_ref,
    ccol,
    crow,
    pair_bias,
    intra,
    pool_w,
    weighted,
    out_buf,
    loc,
    peer_loc,
    chain_in,
    chain_out,
    hand,
    state,
    stats,
    stat_in,
    lse,
    contrib,
    contrib_in,
    loss_out,
    loss_in,
    in_sem,
    out_sem,
    loc_send,
    loc_recv,
    chain_send,
    chain_recv,
    hand_send,
    hand_recv,
    stat_send,
    stat_recv,
    lse_send,
    lse_recv,
    con_send,
    con_recv,
    dp_send,
    dp_recv,
):
    tok, width = x_ref.shape
    heads, _, hd = q_ref.shape
    labels = lq_ref.shape[0]
    recs = lengths_ref.shape[1]
    half_heads = heads // 2
    pairs = n // 2
    scale = hd ** (-0.5)
    soft = scale * LOG2E
    me = lax.axis_index("ctx")
    my_dp = lax.axis_index("dp")
    half = lax.rem(me, 2)
    pair = me // 2
    partner = me + 1 - 2 * half
    even = half == 0

    part = half_heads * hd
    far_cols = pl.ds(pl.multiple_of((1 - half) * part, part), part)
    near_cols = pl.ds(pl.multiple_of(half * part, part), part)
    plan = (
        (lengths_hbm, lengths_ref),
        (decay_hbm, decay_ref),
        (tokens_hbm, x_ref),
        (wk_hbm.at[:, far_cols], wk_ref.at[0]),
        (wv_hbm.at[:, far_cols], wv_ref.at[0]),
        (wk_hbm.at[:, near_cols], wk_ref.at[1]),
        (wv_hbm.at[:, near_cols], wv_ref.at[1]),
        (wq_hbm, wq_ref),
        (lq_hbm, lq_ref),
        (lw_hbm, lw_ref),
        (label_hbm, label_ref),
        (gain_hbm, gain_ref),
    )
    loads = [pltpu.make_async_copy(src, dst, in_sem.at[i]) for i, (src, dst) in enumerate(plan)]
    for load in loads[:5]:
        load.start()

    barrier = pltpu.get_barrier_semaphore()
    for d in range(1, n):
        pl.semaphore_signal(
            barrier,
            inc=1,
            device_id={"ctx": lax.rem(me + d, n)},
            device_id_type=pl.DeviceIdType.MESH,
        )
    for d in range(1, dp_n):
        pl.semaphore_signal(
            barrier,
            inc=1,
            device_id={"dp": lax.rem(my_dp + d, dp_n)},
            device_id_type=pl.DeviceIdType.MESH,
        )

    def send(src, dst, ssem, rsem, where):
        return pltpu.make_async_remote_copy(
            src_ref=src,
            dst_ref=dst,
            send_sem=ssem,
            recv_sem=rsem,
            device_id=where,
            device_id_type=pl.DeviceIdType.MESH,
        )

    loads[0].wait()
    loads[1].wait()
    shard_start = me * tok
    starts = []
    run = jnp.int32(0)
    for r in range(recs):
        starts.append(run)
        run = run + lengths_ref[0, r]

    def record_of(pos):
        rec = jnp.full_like(pos, -1)
        for r in range(recs):
            rec = rec + (starts[r] <= pos).astype(jnp.int32)
        return rec

    def record_scalar(pos):
        rec = jnp.int32(-1)
        for r in range(recs):
            rec = rec + (starts[r] <= pos).astype(jnp.int32)
        return rec

    before_rec = record_scalar(shard_start - 1)
    last_rec = record_scalar(shard_start + tok - 1)

    def col_record(lanes):
        return record_of(shard_start + lax.broadcasted_iota(jnp.int32, (tok, lanes), 0))

    def row_record(rows):
        return record_of(shard_start + lax.broadcasted_iota(jnp.int32, (rows, tok), 1))

    down = lax.broadcasted_iota(jnp.int32, (tok, tok), 0)
    across = lax.broadcasted_iota(jnp.int32, (tok, tok), 1)
    tri_low = (across <= down).astype(F32)
    decays = decay_ref[...]
    cum_rows = (
        lax.dot_general(
            decays, tri_low, NT, precision=lax.Precision.HIGHEST, preferred_element_type=F32
        )
        * LOG2E
    )
    cum_cols = (
        lax.dot_general(
            tri_low, decays, NT, precision=lax.Precision.HIGHEST, preferred_element_type=F32
        )
        * LOG2E
    )
    for h in range(heads):
        crow[h] = cum_rows[h : h + 1, :]
        ccol[h] = jnp.broadcast_to(cum_cols[:, h : h + 1], (tok, hd))
    pair_ok = (across <= down) & (col_record(tok) == row_record(tok))
    pair_bias[...] = jnp.where(pair_ok, math.log2(scale), NEG_FILL)

    def project(w_ref, dst, first):
        columns = w_ref.shape[1]
        step = min(256, columns)
        for c in range(columns // step):
            res = jnp.dot(
                x_ref[...], w_ref[:, c * step : (c + 1) * step], preferred_element_type=F32
            ).astype(BF16)
            for s in range(step // hd):
                dst[first + c * (step // hd) + s] = res[:, s * hd : (s + 1) * hd]

    piece = hd // PIECES

    def local_state(h):
        cum = ccol[h]
        last = cum[tok - 1 : tok, :]
        fade = jnp.exp2(jnp.where(col_record(hd) == last_rec, last - cum, NEG_FILL))
        kdec = (k_ref[h].astype(F32) * fade).astype(BF16)
        made = lax.dot_general(kdec, v_ref[h], TN, preferred_element_type=F32)
        carry = jnp.where(last_rec == before_rec, jnp.exp2(last), 0.0)
        for s in range(PIECES):
            loc[h, s, :piece, :] = made[s * piece : (s + 1) * piece, :]
            loc[h, s, piece:, :] = jnp.broadcast_to(carry, (PAD, hd))

    def loc_copy(i, s):
        h = (1 - half) * half_heads + i
        return send(
            loc.at[h, s],
            peer_loc.at[i, s],
            loc_send.at[i, s],
            loc_recv.at[i, s],
            {"ctx": partner},
        )

    loads[2].wait()
    loads[3].wait()
    for load in loads[5:7]:
        load.start()
    project(wk_ref.at[0], k_ref, (1 - half) * half_heads)
    loads[4].wait()
    for load in loads[7:]:
        load.start()
    project(wv_ref.at[0], v_ref, (1 - half) * half_heads)
    pl.semaphore_wait(barrier, n - 1 + dp_n - 1)

    @pl.when(pair == 0)
    def _():
        chain_in[...] = jnp.zeros_like(chain_in)

    for i in range(half_heads):
        local_state((1 - half) * half_heads + i)
        for s in range(PIECES):
            loc_copy(i, s).start()
    def chain_copy(i, s):
        return send(
            chain_out.at[i, s],
            chain_in.at[i, s],
            chain_send.at[i, s],
            chain_recv.at[i, s],
            {"ctx": lax.rem(me + 2, n)},
        )

    def hand_to(i, s, h):
        return send(
            hand.at[i, s],
            state.at[h, s],
            hand_send.at[i, s],
            hand_recv.at[i, s],
            {"ctx": partner},
        )

    def hand_copy(i, s):
        return hand_to(i, s, half * half_heads + i)

    def hand_arrival(i, s):
        return hand_to(i, s, (1 - half) * half_heads + i)

    def chain_step(i):
        h = half * half_heads + i
        for s in range(PIECES):
            loc_copy(i, s).wait_recv()

            @pl.when(pair > 0)
            def _():
                chain_copy(i, s).wait_recv()

            came = chain_in[i, s]
            own = loc[h, s]
            other = peer_loc[i, s]
            first = jnp.where(even, own, other)
            second = jnp.where(even, other, own)
            middle = first[piece : piece + 1, :] * came + first[:piece, :]

            @pl.when(pair < pairs - 1)
            def _():
                chain_out[i, s] = second[piece : piece + 1, :] * middle + second[:piece, :]
                chain_copy(i, s).start()

            hand[i, s] = jnp.where(even, middle, came)
            hand_copy(i, s).start()
            state[h, s] = jnp.where(even, came, middle)

    loads[5].wait()
    project(wk_ref.at[1], k_ref, half * half_heads)
    loads[6].wait()
    project(wv_ref.at[1], v_ref, half * half_heads)
    for i in range(half_heads):
        local_state(half * half_heads + i)

        @pl.when(pair == 0)
        def _():
            chain_step(i)

    group = 2
    units = heads + heads // group
    first_unit = jnp.where(pair == 0, -half_heads, jnp.minimum(4 * pair - 3, units))

    def maybe_chain(unit):
        i = unit - first_unit

        @pl.when((i >= 0) & (i < half_heads))
        def _():
            chain_step(i)

    loads[7].wait()
    project(wq_ref, q_ref, 0)
    loads[8].wait()

    chunk = min(256, labels)
    members = (
        row_record(16) == lax.broadcasted_iota(jnp.int32, (16, tok), 0)
    ).astype(F32).astype(BF16)

    def pool_unit(h):
        lanes = pl.ds(pl.multiple_of(h * hd, hd), hd)
        rec = col_record(chunk)
        for c in range(labels // chunk):
            cols = slice(c * chunk, (c + 1) * chunk)
            scores = lax.dot_general(
                x_ref[:, lanes], lq_ref[cols, lanes], NT, preferred_element_type=F32
            )
            tops = [
                jnp.max(jnp.where(rec == r, scores, NEG_FILL), axis=0, keepdims=True)
                for r in range(recs)
            ]
            top = tops[0]
            for r in range(1, recs):
                top = jnp.where(rec == r, tops[r], top)
            weight = jnp.exp2((scores - top) * soft).astype(BF16)
            pool_w[h, :, cols] = weight
            for r in range(recs):
                stats[h, r : r + 1, cols] = tops[r] * soft
            mass = jnp.dot(members, weight, preferred_element_type=F32)
            stats[h, recs:, cols] = mass[:recs, :]

    def pool_body(h, _):
        pool_unit(h)
        maybe_chain(h)
        return 0

    lax.fori_loop(0, heads, pool_body, 0)

    def stat_copy(d):
        target = lax.rem(me + d, n)
        return target, send(
            stats.at[lax.rem(target, heads)],
            stat_in.at[me],
            stat_send.at[d],
            stat_recv.at[d],
            {"ctx": target},
        )

    def stat_arrival(d):
        return send(
            stats.at[0],
            stat_in.at[lax.rem(me - d + n, n)],
            stat_send.at[d],
            stat_recv.at[d],
            {"ctx": lax.rem(me + d, n)},
        )

    def each_peer(fn):
        for d in range(1, n):
            fn(d)

    def start_stat(d):
        target, copy = stat_copy(d)

        @pl.when(target < heads)
        def _():
            copy.start()

    each_peer(start_stat)

    def intra_unit(h):
        scores = lax.dot_general(q_ref[h], k_ref[h], NT, preferred_element_type=F32)
        cum = jnp.concatenate([ccol[h]] * (tok // hd), axis=1)
        fade = jnp.exp2(cum - crow[h] + pair_bias[...])
        weights = (scores * fade).astype(BF16)
        intra[h] = jnp.dot(weights, v_ref[h], preferred_element_type=F32)

    def intra_body(u, _):
        for s in range(group):
            intra_unit(u * group + s)
        maybe_chain(heads + u)
        return 0

    lax.fori_loop(0, heads // group, intra_body, 0)

    def lse_copy(d):
        return send(
            lse.at[lax.rem(me, heads)],
            lse.at[lax.rem(me, heads)],
            lse_send.at[d],
            lse_recv.at[d],
            {"ctx": lax.rem(me + d, n)},
        )

    def lse_arrival(d):
        source = lax.rem(me - d + n, n)
        return source, send(
            lse.at[lax.rem(source, heads)],
            lse.at[lax.rem(source, heads)],
            lse_send.at[d],
            lse_recv.at[d],
            {"ctx": lax.rem(me + d, n)},
        )

    @pl.when(me < heads)
    def _():
        stat_in[me] = stats[lax.rem(me, heads)]
        each_peer(lambda d: stat_arrival(d).wait_recv())
        top = stat_in[0, :recs, :]
        for j in range(1, n):
            top = jnp.maximum(top, stat_in[j, :recs, :])
        mass = jnp.zeros_like(top)
        for j in range(n):
            mass = mass + stat_in[j, recs:, :] * jnp.exp2(stat_in[j, :recs, :] - top)
        lse[lax.rem(me, heads)] = top + jnp.log(mass) * LOG2E
        each_peer(lambda d: lse_copy(d).start())

    loads[10].wait()
    hot = (
        lax.broadcasted_iota(jnp.int32, (labels, tok), 0) == label_ref[...]
    ).astype(F32).astype(BF16)
    counts = lax.dot_general(members, hot, NT, preferred_element_type=F32)
    contrib[recs:, :] = counts[:recs, :]

    loads[9].wait()
    loads[11].wait()

    def finish(h):
        lanes = pl.ds(pl.multiple_of(h * hd, hd), hd)
        st = jnp.concatenate([state[h, s] for s in range(PIECES)], axis=0)
        high = st.astype(BF16)
        low = (st - high.astype(F32)).astype(BF16)
        q = q_ref[h]
        inter = jnp.dot(
            jnp.concatenate([q, q], axis=1),
            jnp.concatenate([high, low], axis=0),
            preferred_element_type=F32,
        )
        fade = jnp.exp2(
            jnp.where(col_record(hd) == before_rec, ccol[h] + math.log2(scale), NEG_FILL)
        )
        total = intra[h] + inter * fade
        centred = total - jnp.mean(total, axis=1, keepdims=True)
        variance = jnp.mean(centred * centred, axis=1, keepdims=True)
        rows = (centred * lax.rsqrt(variance + 1e-05) * gain_ref[pl.ds(h, 1), :]).astype(BF16)
        out_buf[:, lanes] = rows
        for c in range(labels // chunk):
            cols = slice(c * chunk, (c + 1) * chunk)
            value = lax.dot_general(rows, lw_ref[cols, lanes], NT, preferred_element_type=F32)
            value = (value * pool_w[h, :, cols].astype(F32)).astype(BF16)
            weighted[h, :, cols] = jnp.dot(members, value, preferred_element_type=F32)[:recs, :]

    for i in range(half_heads + 1):
        if i < half_heads:

            @pl.when(first_unit + i >= units)
            def _():
                chain_step(i)

        if i > 0:
            for s in range(PIECES):
                hand_arrival(i - 1, s).wait_recv()
        if i < half_heads:
            finish(half * half_heads + i)
        if i > 0:
            finish((1 - half) * half_heads + i - 1)

    store = pltpu.make_async_copy(out_buf, out_hbm, out_sem)
    store.start()

    def wait_lse(d):
        source, copy = lse_arrival(d)

        @pl.when(source < heads)
        def _():
            copy.wait_recv()

    each_peer(wait_lse)
    part = jnp.zeros((recs, labels), F32)
    for h in range(heads):
        part = part + weighted[h] * jnp.exp2(stats[h, :recs, :] - lse[h])
    contrib[:recs, :] = part

    def con_copy(d):
        return send(
            contrib,
            contrib_in.at[d],
            con_send.at[d],
            con_recv.at[d],
            {"ctx": lax.rem(me + d, n)},
        )

    each_peer(lambda d: con_copy(d).start())
    contrib_in[0] = contrib[...]
    each_peer(lambda d: con_copy(d).wait_recv())
    both = contrib_in[lax.rem(me, n)]
    for j in range(1, n):
        both = both + contrib_in[lax.rem(me - j + n, n)]
    logits = both[:recs, :]
    logits_ref[...] = logits
    losses = []
    total_loss = jnp.zeros((1, 1), F32)
    for r in range(recs):
        z = logits[r : r + 1, :]
        target = (both[recs + r : recs + r + 1, :] + 0.5) / (
            lengths_ref[0, r].astype(F32) + 1.0
        )
        soft_plus = jnp.maximum(z, 0.0) + jnp.log1p(jnp.exp(-jnp.abs(z)))
        value = jnp.mean(soft_plus - target * z, axis=1, keepdims=True)
        losses.append(value)
        total_loss = total_loss + value
    spot = lax.broadcasted_iota(jnp.int32, (1, recs), 1)
    row = jnp.zeros((1, recs), F32)
    for r in range(recs):
        row = jnp.where(spot == r, losses[r], row)
    loss_ref[...] = row
    loss_out[...] = jnp.broadcast_to(total_loss, loss_out.shape)

    def dp_copy(d):
        return send(
            loss_out,
            loss_in.at[d],
            dp_send.at[d],
            dp_recv.at[d],
            {"dp": lax.rem(my_dp + d, dp_n)},
        )

    for d in range(1, dp_n):
        dp_copy(d).start()
    loss_in[0] = loss_out[...]
    for d in range(1, dp_n):
        dp_copy(d).wait_recv()
    total = loss_in[lax.rem(my_dp, dp_n)]
    for j in range(1, dp_n):
        total = total + loss_in[lax.rem(my_dp - j + dp_n, dp_n)]
    mean_ref[...] = total[:1, :1] / (dp_n * recs)

    for d in range(1, dp_n):
        dp_copy(d).wait_send()
    each_peer(lambda d: con_copy(d).wait_send())

    @pl.when(me < heads)
    def _():
        each_peer(lambda d: lse_copy(d).wait_send())

    def end_stat(d):
        target, copy = stat_copy(d)

        @pl.when(target < heads)
        def _():
            copy.wait_send()

    each_peer(end_stat)
    for i in range(half_heads):
        for s in range(PIECES):
            loc_copy(i, s).wait_send()
            hand_copy(i, s).wait_send()

    @pl.when(pair < pairs - 1)
    def _():
        for i in range(half_heads):
            for s in range(PIECES):
                chain_copy(i, s).wait_send()

    store.wait()


def write_out(*refs):
    ins, outs, held, sems = refs[:4], refs[4:8], refs[8:12], refs[12]
    rows = ins[0].shape[0] // 2
    pieces = [(i, ins[i], outs[i], held[i]) for i in range(1, 4)]
    for p in range(2):
        cut = pl.ds(p * rows, rows)
        pieces.append((4 * p, ins[0].at[cut], outs[0].at[cut], held[0].at[cut]))
    fetches = [pltpu.make_async_copy(src, mid, sems.at[0, i]) for i, src, dst, mid in pieces]
    stores = [pltpu.make_async_copy(mid, dst, sems.at[1, i]) for i, src, dst, mid in pieces]
    for fetch in fetches:
        fetch.start()
    for fetch, store in zip(fetches, stores):
        fetch.wait()
        store.start()
    for store in stores:
        store.wait()


def local(
    tokens,
    log_decay,
    lengths,
    label_ids,
    w_query,
    w_key,
    w_value,
    norm_gain,
    label_query,
    label_weight,
):
    n = lax.axis_size("ctx")
    dp_n = lax.axis_size("dp")
    tok, width = tokens.shape[1:]
    heads = log_decay.shape[1]
    hd = width // heads
    recs = lengths.shape[1]
    labels = label_query.shape[0]
    half = heads // 2
    piece = hd // PIECES
    assert n >= heads and n % 2 == 0
    any_space = pl.BlockSpec(memory_space=pl.ANY)
    hbm = pl.BlockSpec(memory_space=pltpu.HBM)
    vmem = pl.BlockSpec(memory_space=pltpu.VMEM)
    dma = pltpu.SemaphoreType.DMA
    out_shape = (
        jax.ShapeDtypeStruct((tok, width), BF16),
        jax.ShapeDtypeStruct((recs, labels), F32),
        jax.ShapeDtypeStruct((1, recs), F32),
        jax.ShapeDtypeStruct((1, 1), F32),
    )
    results = pl.pallas_call(
        functools.partial(fused, n, dp_n),
        out_shape=out_shape,
        in_specs=[hbm] * 10,
        out_specs=(hbm,) + (vmem,) * 3,
        scratch_shapes=[
            pltpu.SMEM((1, recs), jnp.int32),
            pltpu.VMEM((heads, tok), F32),
            pltpu.VMEM((1, tok), jnp.int32),
            pltpu.VMEM((heads, hd), F32),
            pltpu.VMEM((tok, width), BF16),
            pltpu.VMEM((width, width), BF16),
            pltpu.VMEM((2, width, width // 2), BF16),
            pltpu.VMEM((2, width, width // 2), BF16),
            pltpu.VMEM((labels, width), BF16),
            pltpu.VMEM((labels, width), BF16),
            pltpu.VMEM((heads, tok, hd), BF16),
            pltpu.VMEM((heads, tok, hd), BF16),
            pltpu.VMEM((heads, tok, hd), BF16),
            pltpu.VMEM((heads, tok, hd), F32),
            pltpu.VMEM((heads, 1, tok), F32),
            pltpu.VMEM((tok, tok), F32),
            pltpu.VMEM((heads, tok, hd), F32),
            pltpu.VMEM((heads, tok, labels), BF16),
            pltpu.VMEM((heads, recs, labels), F32),
            pltpu.VMEM((tok, width), BF16),
            pltpu.VMEM((heads, PIECES, piece + PAD, hd), F32),
            pltpu.VMEM((half, PIECES, piece + PAD, hd), F32),
            pltpu.VMEM((half, PIECES, piece, hd), F32),
            pltpu.VMEM((half, PIECES, piece, hd), F32),
            pltpu.VMEM((half, PIECES, piece, hd), F32),
            pltpu.VMEM((heads, PIECES, piece, hd), F32),
            pltpu.VMEM((heads, 2 * recs, labels), F32),
            pltpu.VMEM((n, 2 * recs, labels), F32),
            pltpu.VMEM((heads, recs, labels), F32),
            pltpu.VMEM((2 * recs, labels), F32),
            pltpu.VMEM((n, 2 * recs, labels), F32),
            pltpu.VMEM((8, 128), F32),
            pltpu.VMEM((dp_n, 8, 128), F32),
            dma((12,)),
            dma,
            dma((half, PIECES)),
            dma((half, PIECES)),
            dma((half, PIECES)),
            dma((half, PIECES)),
            dma((half, PIECES)),
            dma((half, PIECES)),
            dma((n,)),
            dma((n,)),
            dma((n,)),
            dma((n,)),
            dma((n,)),
            dma((n,)),
            dma((dp_n,)),
            dma((dp_n,)),
        ],
        compiler_params=pltpu.CompilerParams(
            collective_id=0, has_side_effects=True, vmem_limit_bytes=VMEM_LIMIT
        ),
    )(
        lengths,
        log_decay[0],
        label_ids,
        norm_gain.reshape(heads, hd),
        tokens[0],
        w_query,
        w_key,
        w_value,
        label_query,
        label_weight,
    )
    out, logits, loss, mean = pl.pallas_call(
        write_out,
        out_shape=out_shape,
        in_specs=[any_space] * 4,
        out_specs=(hbm,) * 4,
        scratch_shapes=[pltpu.VMEM(o.shape, o.dtype) for o in out_shape] + [dma((2, 5))],
        compiler_params=pltpu.CompilerParams(vmem_limit_bytes=VMEM_LIMIT),
    )(*results)
    return (out[None], logits[None], loss, mean.reshape(()))


def solution(mesh):
    return jax.shard_map(
        local,
        mesh=mesh,
        in_specs=(
            P("dp", "ctx", None),
            P("dp", None, "ctx"),
            P("dp", None),
            P("dp", "ctx"),
            P(),
            P(),
            P(),
            P(),
            P(),
            P(),
        ),
        out_specs=(P("dp", "ctx", None), P("dp", None, None), P("dp", None), P()),
        check_vma=False,
    )
```
